32 devices in a mesh: dp: 4 (over x, core), blk: 8 (over z, y).
Axes of the slice: x: 2, y: 2, z: 4, core: 2. Of those that a mesh axis runs over, the one named last changes fastest.
Arguments:
- hidden: bfloat16 [4096, 1536], P(('dp', 'blk')), may hold values from -6 to 6
- segments: int32 [4096], P(('dp', 'blk')), may hold values from 0 to 1, as said below
- positions: int32 [3, 4096], P(None, ('dp', 'blk')), may hold values from 0 to 63
- condition: float32 [8, 1024], P('dp'), may hold values from -6 to 6
- captions: bfloat16 [8, 128, 4096], P('dp', None, 'blk'), may hold values from -6 to 6
- dropped: int32 [8], P('dp'), may hold values from 0 to 1, as said below
- null_caption: bfloat16 [128, 4096], P(None, 'blk'), may hold values from -6 to 6
- ada_weight: bfloat16 [1024, 6144], P('blk'), may hold values from -0.1875 to 0.1875
- ada_bias: float32 [6144], replicated, may hold values from -1.5 to 1.5
- qkv_weight: bfloat16 [1536, 4608], P('blk'), may hold values from -0.15625 to 0.15625
- out_weight: bfloat16 [1536, 1536], P('blk'), may hold values from -0.15625 to 0.15625
- caption_weight: bfloat16 [4096, 3072], P('blk'), may hold values from -0.09375 to 0.09375
- gate_up: bfloat16 [1536, 8192], P('blk'), may hold values from -0.15625 to 0.15625
- down_weight: bfloat16 [4096, 1536], P('blk'), may hold values from -0.09375 to 0.09375
- gains: float32 [7, 1536], replicated, may hold values from 0.5 to 1.5
- head_gate: float32 [24], replicated, may hold values from 0.3 to 1
- cotangent: bfloat16 [4096, 1536], P(('dp', 'blk')), may hold values from -6 to 6
Outputs:
- output: float32 [4096, 1536], P(('dp', 'blk'))
- input_grad: float32 [4096, 1536], P(('dp', 'blk'))
- ada_weight_grad: float32 [1024, 6144], P('blk')
- ada_bias_grad: float32 [6144], replicated
- qkv_grad: float32 [1536, 4608], P('blk')
- out_grad: float32 [1536, 1536], P('blk')
- caption_grad: float32 [4096, 3072], P('blk')
- gate_up_grad: float32 [1536, 8192], P('blk')
- down_grad: float32 [4096, 1536], P('blk')
- null_grad: float32 [128, 4096], P(None, 'blk')
- gains_grad: float32 [7, 1536], replicated
- head_gate_grad: float32 [24], replicated
The draws below stay inside these ranges and needn't reach their ends.
Inputs may be any that keep to these rules, and one draw needn't show every extreme that they name: `segments`: within each group of 1024 tokens the clip numbers never fall and each of the 2 clips holds one token or more. Some clip is dropped and some is kept.
All inputs are finite; a program needn't handle non-finite values.
Results may differ from the reference program's by a relative error of at most 0.039.
Values may be sent and summed in bfloat16 or wider, within the bound.
No kernel may reach another device: no remote copies, remote signals or barrier semaphores. Data moves between devices by JAX's collectives and lax.ppermute only.
A program may use at most 320 MiB of HBM per device.

```python
import math
import jax
import jax.numpy as jnp
from jax import lax

HEADS = 24
HEAD = 64
D = 1536
FF = 4096
TEXT = 4096
COND = 1024
CAP = 128
CLIPS = 2
TOK_DEV = 128
SEQ = 1024
TOKENS_ALL = 4096
CLIPS_ALL = 8


def draw_segments(key, part):
    key = jax.random.fold_in(key, 17)
    group_count = TOKENS_ALL // SEQ
    group_keys = jax.random.split(key, group_count)

    def one_group(group_key):
        offset = jax.random.randint(group_key, (), 1, TOK_DEV)
        side = jax.random.randint(jax.random.fold_in(group_key, 3), (), 0, 2)
        cut = jnp.where(side == 1, SEQ - offset, offset)
        return (jnp.arange(SEQ) >= cut).astype(jnp.int32)
    return jax.vmap(one_group)(group_keys).reshape(-1).astype(jnp.int32)


def draw_dropped(key, part):
    key = jax.random.fold_in(key, 29)
    flags = jax.random.randint(key, (CLIPS_ALL,), 0, 2)
    picked = jax.random.permutation(jax.random.fold_in(key, 5), CLIPS_ALL)
    flags = flags.at[picked[0]].set(1)
    flags = flags.at[picked[1]].set(0)
    return flags.astype(jnp.int32)


def place_ends(array, own_key, low, high):
    extent = array.shape
    place = [jax.random.randint(jax.random.fold_in(own_key, axis), (), 0, extent[axis]) for axis in range(len(extent))]
    array = array.at[tuple(place)].set(low)
    longest = extent.index(max(extent))
    place[longest] = (place[longest] + 1) % extent[longest]
    return array.at[tuple(place)].set(high)


def block_scale(stream_key, shape, cuts, least, largest):
    level = 1.0
    for dim, blocks in cuts:
        draws = jax.random.uniform(jax.random.fold_in(jax.random.fold_in(stream_key, 6), dim), (blocks,), jnp.float32, least / len(cuts), largest / len(cuts))
        level = level * jnp.repeat(jnp.exp(draws), shape[dim] // blocks).reshape((-1,) + (1,) * (len(shape) - 1 - dim))
    return level


def centred(own_key, shape, deviation, reach, pieces=(), kind=jnp.bfloat16):
    values = deviation * jax.random.normal(own_key, shape, jnp.float32)
    if pieces:
        values = values * block_scale(own_key, shape, pieces, -0.22, 0.18)
    return jnp.clip(values, -reach, reach).astype(kind)


def setup_inputs(seed: int = 0) -> dict:
    seeds = jax.random.split(jax.random.key(seed), 18)
    hidden = centred(seeds[0], (TOKENS_ALL, D), 1.0, 6.0, ((0, 32),))
    segments = draw_segments(jax.random.fold_in(seeds[17], 71), 0)
    positions = place_ends(jax.random.randint(seeds[2], (3, TOKENS_ALL), 0, 64), jax.random.fold_in(seeds[2], 1), 0, 63).astype(jnp.int32)
    condition = centred(seeds[3], (CLIPS_ALL, COND), 1.0, 6.0, ((0, 4),), jnp.float32)
    captions = centred(seeds[4], (CLIPS_ALL, CAP, TEXT), 1.0, 6.0, ((0, 4), (2, 8)))
    dropped = draw_dropped(jax.random.fold_in(seeds[17], 71), 0)
    null_caption = centred(seeds[6], (CAP, TEXT), 1.0, 6.0, ((1, 8),))
    ada_weight = centred(seeds[7], (COND, 4 * D), COND ** -0.5, 0.1875, ((0, 8),))
    ada_bias = centred(seeds[8], (4 * D,), 0.3, 1.5, (), jnp.float32)
    qkv_weight = centred(seeds[9], (D, 3 * D), D ** -0.5, 0.15625, ((0, 8),))
    out_weight = centred(seeds[10], (D, D), D ** -0.5, 0.15625, ((0, 8),))
    caption_weight = centred(seeds[11], (TEXT, 2 * D), TEXT ** -0.5, 0.09375, ((0, 8),))
    gate_up = centred(seeds[12], (D, 2 * FF), D ** -0.5, 0.15625, ((0, 8),))
    down_weight = centred(seeds[13], (FF, D), FF ** -0.5, 0.09375, ((0, 8),))
    gains = jnp.clip(1.0 + 0.1 * jax.random.normal(seeds[14], (7, D), jnp.float32), 0.5, 1.5)
    head_gate = jnp.clip(jax.random.uniform(seeds[15], (HEADS,), jnp.float32, 0.3, 1.0), 0.3, 1.0)
    cotangent = centred(seeds[16], (TOKENS_ALL, D), 1.0, 6.0, ((0, 32),))
    return dict(hidden=hidden, segments=segments, positions=positions, condition=condition, captions=captions, dropped=dropped, null_caption=null_caption, ada_weight=ada_weight, ada_bias=ada_bias, qkv_weight=qkv_weight, out_weight=out_weight, caption_weight=caption_weight, gate_up=gate_up, down_weight=down_weight, gains=gains, head_gate=head_gate, cotangent=cotangent)


PRECISE = lax.Precision.HIGHEST
EPSILON = 1e-06
NEGATIVE = -1e+30

@jax.custom_vjp
def low(v):
    return lax.optimization_barrier(v.astype(jnp.bfloat16)).astype(jnp.float32)

@jax.custom_vjp
def low_back(v):
    return v

def low_keep(v):
    return (low(v), None)

def low_pass(kept, grad):
    return (grad,)

def back_keep(v):
    return (v, None)

def back_low(kept, grad):
    return (low(grad),)
low.defvjp(low_keep, low_pass)
low_back.defvjp(back_keep, back_low)

def norm_rows(values, gain):
    return values * lax.rsqrt(lax.optimization_barrier(jnp.mean(values * values, -1, keepdims=True)) + EPSILON) * gain

def rope_tables(positions):
    pair_count = HEAD // 2
    pair_index = jnp.arange(pair_count)
    frequency = 10000.0 ** (-3.0 * (pair_index // 3).astype(jnp.float32) / pair_count)
    select = ((pair_index % 3)[None, :] == jnp.arange(3)[:, None]).astype(jnp.float32)
    angles = jnp.dot(positions.astype(jnp.float32).T, select, precision=PRECISE) * frequency[None, :]
    return (jnp.cos(angles), jnp.sin(angles))

def rotate(tensor, cosine_table, sine_table, sign):
    row_count = tensor.shape[0]
    paired = tensor.reshape(row_count, -1, cosine_table.shape[1], 2)
    even_part = paired[..., 0]
    odd_part = paired[..., 1]
    cosines = cosine_table[:, None, :]
    sines = sign * sine_table[:, None, :]
    turned = jnp.stack([even_part * cosines - odd_part * sines, even_part * sines + odd_part * cosines], -1)
    return turned.reshape(row_count, -1)

def attend(query_heads, key_heads, value_heads, allowed):
    scaling = HEAD ** (-0.5)
    scores = low_back(jnp.einsum('qhd,khd->hqk', query_heads, key_heads, precision=PRECISE) * scaling)
    masked = jnp.where(allowed, scores, NEGATIVE)
    row_top = lax.optimization_barrier(jnp.max(masked, -1, keepdims=True))
    exp_scores = jnp.where(allowed, jnp.exp(masked - row_top), 0.0)
    totals = lax.optimization_barrier(jnp.sum(exp_scores, -1))
    return jnp.einsum('hqk,khd->qhd', low(exp_scores), value_heads, precision=PRECISE) / totals.T[:, :, None]

def self_attention(queries, key_rows, value_rows, seg_rows):
    row_count = queries.shape[0]
    span_rows = math.gcd(row_count, 512)
    query_blocks = queries.reshape(row_count // span_rows, span_rows, HEADS, HEAD)
    seg_blocks = seg_rows.reshape(row_count // span_rows, span_rows)
    key_heads = key_rows.reshape(row_count, HEADS, HEAD)
    value_heads = value_rows.reshape(row_count, HEADS, HEAD)

    def per_block(inputs):
        query_block, seg_block = inputs
        allowed = (seg_block[:, None] == seg_rows[None, :])[None]
        return attend(query_block, key_heads, value_heads, allowed)
    attended = lax.map(jax.checkpoint(per_block), (query_blocks, seg_blocks))
    return attended.reshape(row_count, HEADS * HEAD)

def cross_attention(queries, caption_keys, caption_values, seg_rows):
    row_count = queries.shape[0]
    key_heads = caption_keys.reshape(-1, HEADS, HEAD)
    value_heads = caption_values.reshape(-1, HEADS, HEAD)
    key_clip = jnp.arange(key_heads.shape[0]) // CAP
    allowed = (seg_rows[:, None] == key_clip[None, :])[None]
    attended = attend(queries.reshape(row_count, HEADS, HEAD), key_heads, value_heads, allowed)
    return attended.reshape(row_count, HEADS * HEAD)

def group_forward(weights, source, seg_rows, positions, condition, captions, dropped):
    ada_weight, ada_bias, qkv_weight, out_weight, caption_weight, gate_up, down_weight, null_caption, gains, head_gate = weights
    modulation = low_back(jnp.dot(low(jax.nn.silu(condition)), ada_weight, precision=PRECISE)) + ada_bias
    chosen = jnp.where(dropped[:, None, None] == 1, null_caption[None], captions).reshape(CLIPS * CAP, TEXT)
    caption_proj = low_back(jnp.dot(chosen, caption_weight, precision=PRECISE))
    caption_keys = low(norm_rows(caption_proj[:, :D], gains[6]))
    caption_values = low(caption_proj[:, D:])
    onehot = (seg_rows[:, None] == jnp.arange(CLIPS)[None, :]).astype(jnp.float32)
    token_mod = jnp.dot(onehot, modulation, precision=PRECISE)
    first_in = low(norm_rows(source, gains[0]) * (1.0 + token_mod[:, :D]))
    projected = low_back(jnp.dot(first_in, qkv_weight, precision=PRECISE))
    cosine_table, sine_table = rope_tables(positions)
    queries = low(rotate(norm_rows(projected[:, :D], gains[4]), cosine_table, sine_table, 1.0))
    key_rows = low(rotate(norm_rows(projected[:, D:2 * D], gains[5]), cosine_table, sine_table, 1.0))
    value_rows = low(projected[:, 2 * D:])
    out_self = self_attention(queries, key_rows, value_rows, seg_rows)
    out_cross = low_back(cross_attention(queries, caption_keys, caption_values, seg_rows))
    head_scale = jnp.repeat(jnp.tanh(head_gate), HEAD)
    mixed_heads = low(low_back(out_self + head_scale[None, :] * out_cross))
    attended = low_back(jnp.dot(mixed_heads, out_weight, precision=PRECISE))
    middle = source + jnp.tanh(token_mod[:, D:2 * D]) * norm_rows(attended, gains[1])
    second_in = low(norm_rows(middle, gains[2]) * (1.0 + token_mod[:, 2 * D:3 * D]))
    gate_values = low_back(jnp.dot(second_in, gate_up, precision=PRECISE))
    activated = low(jax.nn.silu(gate_values[:, :FF]) * gate_values[:, FF:])
    lowered = low_back(jnp.dot(activated, down_weight, precision=PRECISE))
    return middle + jnp.tanh(token_mod[:, 3 * D:]) * norm_rows(lowered, gains[3])

def reference(hidden, segments, positions, condition, captions, dropped, null_caption, ada_weight, ada_bias, qkv_weight, out_weight, caption_weight, gate_up, down_weight, gains, head_gate, cotangent):
    weights = (ada_weight.astype(jnp.float32), ada_bias, qkv_weight.astype(jnp.float32), out_weight.astype(jnp.float32), caption_weight.astype(jnp.float32), gate_up.astype(jnp.float32), down_weight.astype(jnp.float32), null_caption.astype(jnp.float32), gains, head_gate)
    groups = condition.shape[0] // CLIPS
    seg_groups = segments.reshape(groups, -1)
    pos_groups = positions.reshape(3, groups, -1).transpose(1, 0, 2)
    cond_groups = condition.reshape(groups, CLIPS, COND)
    caption_groups = captions.astype(jnp.float32).reshape(groups, CLIPS, CAP, TEXT)
    drop_groups = dropped.reshape(groups, CLIPS)

    def forward(weights, source):
        grouped = source.reshape(groups, -1, D)

        def per_group(inputs):
            return group_forward(weights, *inputs)
        result = lax.map(per_group, (grouped, seg_groups, pos_groups, cond_groups, caption_groups, drop_groups))
        return result.reshape(-1, D)
    output, pullback = jax.vjp(forward, weights, hidden.astype(jnp.float32))
    gradients, input_grad = pullback(cotangent.astype(jnp.float32))
    return (output, input_grad, gradients[0], gradients[1], gradients[2], gradients[3], gradients[4], gradients[5], gradients[6], gradients[7], gradients[8], gradients[9])
```

```python
import functools

import jax
import jax.numpy as jnp
from jax import lax
from jax.experimental import pallas as pl
from jax.experimental.pallas import tpu as pltpu
from jax.sharding import Mesh, PartitionSpec as P

HEADS = 24
HEAD = 64
D = 1536
FF = 4096
CAP = 128
CLIPS = 2
PAIR = 2 * HEAD

PRECISE = lax.Precision.HIGHEST
EPSILON = 1e-06
NEGATIVE = -1e30
F32 = jnp.float32
LOW = jnp.bfloat16
SWAP = [(0, 1), (1, 0)]


def inv_root(values):
    return lax.rsqrt(jnp.mean(values * values, -1, keepdims=True) + EPSILON)


def unit_rows(values):
    return values * inv_root(values)


def norm_back(grad_in, values, gain):
    root = inv_root(values)
    normed = values * root
    inner = grad_in * gain
    back = root * (inner - normed * jnp.mean(inner * normed, -1, keepdims=True))
    return back, jnp.sum(grad_in * normed, 0)


def rounded(values):
    return lax.reduce_precision(values, 8, 7)


def low(values):
    return rounded(values).astype(LOW)


def dot(a, b, dims=((1,), (0,))):
    return lax.dot_general(a, b, (dims, ((), ())), preferred_element_type=F32)


def nt(a, b):
    return lax.dot_general(a, b, (((1,), (1,)), ((), ())), preferred_element_type=F32)


def tn(a, b):
    return lax.dot_general(a, b, (((0,), (0,)), ((), ())), preferred_element_type=F32)


def nn(a, b):
    return lax.dot_general(a, b, (((1,), (0,)), ((), ())), preferred_element_type=F32)


def cross_bias(seg_col, count):
    clip = lax.broadcasted_iota(jnp.int32, (1, count), 1) // CAP
    return jnp.where(seg_col == clip, 0.0, NEGATIVE)


def forward_near(q_ref, k_ref, v_ref, ck_ref, cv_ref, sq_ref, sk_ref, o_ref, oc_ref, st_ref):
    seg_col = sq_ref[...]
    bias = jnp.where(seg_col == sk_ref[...], 0.0, NEGATIVE)
    bias_cross = cross_bias(seg_col, ck_ref.shape[0])
    for h in range(2):
        at = slice(h * HEAD, (h + 1) * HEAD)
        q = q_ref[:, at]
        s = nt(q, k_ref[:, at]) + bias
        m = jnp.max(s, -1, keepdims=True)
        e = jnp.exp(s - m)
        st_ref[0, :, h : h + 1] = m
        st_ref[0, :, 2 + h : 3 + h] = jnp.sum(e, -1, keepdims=True)
        o_ref[:, at] = nn(e.astype(LOW), v_ref[:, at])
        s = nt(q, ck_ref[:, at]) + bias_cross
        m = jnp.max(s, -1, keepdims=True)
        e = jnp.exp(s - m)
        total = jnp.sum(e, -1, keepdims=True)
        st_ref[0, :, 4 + h : 5 + h] = m + jnp.log(total)
        oc_ref[:, at] = nn(e.astype(LOW), cv_ref[:, at]) / total


def forward_far(
    count, q_ref, k_ref, v_ref, sq_ref, sk_ref, o_ref, oc_ref, st_ref, gate_ref, os_ref, mix_ref, lse_ref, m_ref, l_ref
):
    step = pl.program_id(1)

    @pl.when(step == 0)
    def _():
        os_ref[...] = o_ref[...]
        m_ref[...] = st_ref[0, :, 0:2]
        l_ref[...] = st_ref[0, :, 2:4]

    bias = jnp.where(sq_ref[...] == sk_ref[0], 0.0, NEGATIVE)
    for h in range(2):
        at = slice(h * HEAD, (h + 1) * HEAD)
        s = nt(q_ref[:, at], k_ref[0, :, at]) + bias
        before = m_ref[:, h : h + 1]
        m = jnp.maximum(before, jnp.max(s, -1, keepdims=True))
        e = jnp.exp(s - m)
        factor = jnp.exp(before - m)
        m_ref[:, h : h + 1] = m
        l_ref[:, h : h + 1] = l_ref[:, h : h + 1] * factor + jnp.sum(e, -1, keepdims=True)
        os_ref[:, at] = os_ref[:, at] * factor + nn(e.astype(LOW), v_ref[0, :, at])

    @pl.when(step == count - 1)
    def _():
        for h in range(2):
            at = slice(h * HEAD, (h + 1) * HEAD)
            total = l_ref[:, h : h + 1]
            out = os_ref[:, at] / total
            os_ref[:, at] = out
            mix_ref[:, at] = (out + gate_ref[:, at] * oc_ref[:, at]).astype(LOW)
            lse_ref[0, :, h : h + 1] = m_ref[:, h : h + 1] + jnp.log(total)


def backward_far(
    q_ref, g_ref, os_ref, oc_ref, lse_ref, st_ref, gate_ref, k_ref, v_ref, ck_ref, cv_ref, sq_ref, sk_ref,
    dq_ref, dk_ref, dv_ref, dck_ref, dcv_ref, dh_ref, delta_ref,
):
    step = pl.program_id(1)
    seg_col = sq_ref[...]
    scaling = HEAD**-0.5

    @pl.when(step == 0)
    def _():
        bias_cross = cross_bias(seg_col, ck_ref.shape[0])
        g = g_ref[...].astype(F32)
        dh_ref[...] = jnp.sum(g * oc_ref[...], 0, keepdims=True)
        for h in range(2):
            at = slice(h * HEAD, (h + 1) * HEAD)
            gh = g[:, at]
            delta_ref[0, :, h : h + 1] = jnp.sum(gh * os_ref[:, at], -1, keepdims=True)
            gc = (gate_ref[:, at] * gh).astype(LOW)
            delta = jnp.sum(gc.astype(F32) * oc_ref[:, at], -1, keepdims=True)
            q = q_ref[:, at]
            p = jnp.exp(nt(q, ck_ref[:, at]) + bias_cross - st_ref[0, :, 4 + h : 5 + h])
            ds = (p * (nt(gc, cv_ref[:, at]) - delta)).astype(LOW)
            dq_ref[:, at] = nn(ds, ck_ref[:, at]) * scaling
            dck_ref[:, at] = tn(ds, q).astype(dck_ref.dtype)
            dcv_ref[:, at] = tn(p.astype(LOW), gc).astype(dcv_ref.dtype)

    bias = jnp.where(seg_col == sk_ref[0], 0.0, NEGATIVE)
    for h in range(2):
        at = slice(h * HEAD, (h + 1) * HEAD)
        q = q_ref[:, at]
        g = g_ref[:, at]
        k = k_ref[0, :, at]
        p = jnp.exp(nt(q, k) + bias - lse_ref[0, :, h : h + 1])
        ds = (p * (nt(g, v_ref[0, :, at]) - delta_ref[0, :, h : h + 1])).astype(LOW)
        dq_ref[:, at] += nn(ds, k) * scaling
        dk_ref[0, :, at] = tn(ds, q).astype(dk_ref.dtype)
        dv_ref[0, :, at] = tn(p.astype(LOW), g).astype(dv_ref.dtype)


def backward_near(q_ref, g_ref, lse_ref, delta_ref, k_ref, v_ref, sq_ref, sk_ref, dp_ref, dq_ref, dk_ref, dv_ref):
    bias = jnp.where(sq_ref[...] == sk_ref[...], 0.0, NEGATIVE)
    scaling = HEAD**-0.5
    for h in range(2):
        at = slice(h * HEAD, (h + 1) * HEAD)
        q = q_ref[:, at]
        g = g_ref[:, at]
        k = k_ref[:, at]
        p = jnp.exp(nt(q, k) + bias - lse_ref[0, :, h : h + 1])
        ds = (p * (nt(g, v_ref[:, at]) - delta_ref[0, :, h : h + 1])).astype(LOW)
        dq_ref[:, at] = dp_ref[:, at] + nn(ds, k) * scaling
        dk_ref[:, at] = tn(ds, q)
        dv_ref[:, at] = tn(p.astype(LOW), g)


def attention_calls(tokens, width, capt, far):
    pairs = width // PAIR
    sds = jax.ShapeDtypeStruct

    def cols(rows):
        return pl.BlockSpec((rows, PAIR), lambda i, *r: (0, i))

    def stat(n):
        return pl.BlockSpec((1, tokens, n), lambda i, *r: (i, 0, 0))

    seg_col = pl.BlockSpec((tokens, 1), lambda i, *r: (0, 0))
    seg_row = pl.BlockSpec((1, tokens), lambda i, *r: (0, 0))
    far_cols = pl.BlockSpec((1, tokens, PAIR), lambda i, r: (r, 0, i))
    far_row = pl.BlockSpec((1, 1, tokens), lambda i, r: (r, 0, 0))
    gate = cols(1)
    tok, cap = cols(tokens), cols(capt)

    def cost(keys, products):
        return pl.CostEstimate(
            flops=2 * tokens * keys * width * products,
            bytes_accessed=8 * tokens * width * 4,
            transcendentals=tokens * keys * (width // HEAD),
        )

    params = pltpu.CompilerParams(vmem_limit_bytes=48 * 1024 * 1024)
    near = pl.pallas_call(
        forward_near,
        grid=(pairs,),
        in_specs=[tok, tok, tok, cap, cap, seg_col, seg_row],
        out_specs=[tok, tok, stat(8)],
        out_shape=[sds((tokens, width), F32), sds((tokens, width), F32), sds((pairs, tokens, 8), F32)],
        compiler_params=params,
        cost_estimate=cost(tokens + capt, 2),
        name="attn_near",
    )
    away = pl.pallas_call(
        functools.partial(forward_far, far),
        grid=(pairs, far),
        in_specs=[tok, far_cols, far_cols, seg_col, far_row, tok, tok, stat(8), gate],
        out_specs=[tok, tok, stat(2)],
        out_shape=[sds((tokens, width), F32), sds((tokens, width), LOW), sds((pairs, tokens, 2), F32)],
        scratch_shapes=[pltpu.VMEM((tokens, 2), F32), pltpu.VMEM((tokens, 2), F32)],
        compiler_params=params,
        cost_estimate=cost(tokens * far, 2),
        name="attn_far",
    )
    back_away = pl.pallas_call(
        backward_far,
        grid=(pairs, far),
        in_specs=[tok, tok, tok, tok, stat(2), stat(8), gate, far_cols, far_cols, cap, cap, seg_col, far_row],
        out_specs=[tok, far_cols, far_cols, cap, cap, gate, stat(2)],
        out_shape=[
            sds((tokens, width), F32),
            sds((far, tokens, width), LOW),
            sds((far, tokens, width), LOW),
            sds((capt, width), F32),
            sds((capt, width), F32),
            sds((1, width), F32),
            sds((pairs, tokens, 2), F32),
        ],
        compiler_params=params,
        cost_estimate=cost(tokens * far + capt, 5),
        name="attn_back_far",
    )
    back_near = pl.pallas_call(
        backward_near,
        grid=(pairs,),
        in_specs=[tok, tok, stat(2), stat(2), tok, tok, seg_col, seg_row, tok],
        out_specs=[tok, tok, tok],
        out_shape=[sds((tokens, width), F32)] * 3,
        compiler_params=params,
        cost_estimate=cost(tokens, 5),
        name="attn_back_near",
    )
    return near, away, back_away, back_near


def swap(value, axis):
    return lax.ppermute(value, axis, SWAP)


def pair_stack(value, axis, dim):
    other = swap(value, axis)
    first = lax.axis_index(axis) == 0
    return jnp.concatenate([jnp.where(first, value, other), jnp.where(first, other, value)], dim)


def pair_reduce(value, axis, dim):
    half = value.shape[dim] // 2
    me = lax.axis_index(axis)
    sent = lax.dynamic_slice_in_dim(value, (1 - me) * half, half, dim).astype(LOW)
    kept = lax.dynamic_slice_in_dim(value, me * half, half, dim)
    return kept.astype(F32) + swap(sent, axis).astype(F32)


def on_device(
    far_count,
    lead,
    hidden,
    segments,
    positions,
    condition,
    captions,
    dropped,
    null_caption,
    ada_weight,
    ada_bias,
    qkv_weight,
    out_weight,
    caption_weight,
    gate_up,
    down_weight,
    gains,
    head_gate,
    cotangent,
):
    outer = far_count
    me_c = lax.axis_index("p") * 2 + lax.axis_index("y")
    me_o = lax.axis_index("o")
    core = lax.axis_index("core")
    me_x = lax.axis_index("x")
    me_b = lax.axis_index(("p", "y", "o") if lead else ("o", "p", "y"))
    tokens = hidden.shape[0]
    square = 4 * tokens
    width = D // 4

    def blocks(value):
        rest = value.shape[-1] // (4 * outer)
        if lead:
            return value.reshape(value.shape[:-1] + (4, outer, rest)).swapaxes(-3, -2)
        return value.reshape(value.shape[:-1] + (outer, 4, rest))

    def unblocks(value):
        if lead:
            value = value.swapaxes(-3, -2)
        return value.reshape(value.shape[:-3] + (-1,))

    def row_blocks(value):
        rest = value.shape[0] // (4 * outer)
        if lead:
            return value.reshape((4, outer, rest) + value.shape[1:]).swapaxes(0, 1)
        return value.reshape((outer, 4, rest) + value.shape[1:])

    def row_unblocks(value):
        if lead:
            value = value.swapaxes(0, 1)
        return value.reshape((-1,) + value.shape[3:])

    def my_cols(value):
        mine = lax.dynamic_index_in_dim(blocks(value), me_c, value.ndim, keepdims=False)
        return mine.reshape(value.shape[:-1] + (-1,))

    def put_cols(value):
        split = value.reshape(value.shape[:-1] + (outer, 1, value.shape[-1] // outer))
        here = (jnp.arange(4) == me_c).reshape(4, 1)
        return unblocks(jnp.where(here, split, 0.0))

    def outer_stack(value):
        if outer == 2:
            return pair_stack(value[None], "o", 0)
        return lax.all_gather(value, "o", axis=0)

    def outer_reduce(value):
        if outer == 2:
            return pair_reduce(value, "o", 0)[0]
        return lax.psum_scatter(value.astype(LOW), "o", scatter_dimension=0).astype(F32)

    def outer_sum(value):
        if outer == 2:
            return rounded(value) + swap(low(value), "o").astype(F32)
        return lax.psum(low(value), "o").astype(F32)

    def outer_sum_wide(value):
        if outer == 2:
            return value + swap(value, "o")
        return lax.psum(value, "o")

    def far(value):
        return jnp.stack([lax.ppermute(value, "o", [(i, i ^ r) for i in range(outer)]) for r in range(1, outer)])

    def far_back(value):
        total = 0.0
        for r in range(1, outer):
            total = total + lax.ppermute(value[r - 1], "o", [(i, i ^ r) for i in range(outer)]).astype(F32)
        return total

    def gather_square(rows):
        half = rows.shape[0] // 2
        a, b = rows[:half], rows[half:]
        ya, pb = swap(a, "y"), swap(b, "p")
        pa = swap(jnp.concatenate([a, ya]), "p")
        yb = swap(jnp.concatenate([b, pb]), "y")
        return jnp.concatenate([a, b, ya, yb[:half], pa[:half], pb, pa[half:], yb[half:]])

    def scatter_square(full):
        count = full.shape[0] // 4
        half = count // 2
        a = [full[i * count : i * count + half] for i in range(4)]
        b = [full[i * count + half : (i + 1) * count] for i in range(4)]
        ra = swap(jnp.concatenate([a[2], a[3]]).astype(LOW), "p").astype(F32)
        rb = swap(jnp.concatenate([b[1], b[3]]).astype(LOW), "y").astype(F32)
        a0 = a[0] + ra[:half] + swap((a[1] + ra[half:]).astype(LOW), "y").astype(F32)
        b0 = b[0] + rb[:half] + swap((b[2] + rb[half:]).astype(LOW), "p").astype(F32)
        return jnp.concatenate([a0, b0])

    def square_exchange(value):
        result = jnp.zeros_like(value)
        for r, axes in ((0, ()), (1, ("y",)), (2, ("p",)), (3, ("p", "y"))):
            piece = lax.dynamic_slice_in_dim(value, me_c ^ r, 1, 0)
            if r:
                piece = lax.ppermute(piece, axes if r == 3 else axes[0], [(i, i ^ r) for i in range(4)] if r == 3 else SWAP)
            result = lax.dynamic_update_slice_in_dim(result, piece, me_c ^ r, 0)
        return result

    def square_sum(own_rows, shared):
        count = own_rows.shape[0]
        split = own_rows.reshape(count, 4, -1)
        width_in = split.shape[2]
        whole = jnp.concatenate([split.reshape(count * 4, width_in), shared.reshape(-1, width_in)])
        for axis, order in (("y", (1, 0, 3, 2)), ("p", (2, 3, 0, 1))):
            other = swap(whole, axis)
            order = [4 * i + j for i in range(count) for j in order]
            whole = whole + jnp.concatenate([other[i : i + 1] for i in order] + [other[count * 4 :]])
        return whole[: count * 4].reshape(count, -1), whole[count * 4 :].reshape(-1)

    def group_sum(value):
        value = rounded(value) + swap(low(value), "y").astype(F32)
        value = rounded(value) + swap(low(value), "p").astype(F32)
        return outer_sum(value)

    def all_dp(value):
        return pair_stack(pair_stack(value[None], "x", 0)[None], "core", 0)

    def fetch_qkv(weight):
        quarter = weight.shape[0] // 4
        mine = lax.dynamic_slice_in_dim(weight, (me_x * 2 + core) * quarter, quarter, 0)
        sent = jnp.moveaxis(blocks(mine.reshape(quarter, 3, D)), -2, 0)
        part = outer_stack(square_exchange(sent.reshape(4, quarter, -1)))
        part = pair_stack(part[None], "x", 0)
        other = swap(part, "core")
        whole = jnp.stack([jnp.where(core == i, part, other) for i in range(2)], 1)
        whole = whole.transpose(2, 3, 0, 1, 4, 5)
        return row_unblocks(whole.reshape(whole.shape[:2] + (4 * quarter, whole.shape[-1])))

    def fetch_rows(weight):
        quarter = weight.shape[1] // 4
        mine = lax.dynamic_slice_in_dim(weight, (core * 2 + me_x) * quarter, quarter, 1)
        part = outer_stack(mine).reshape(outer * weight.shape[0], quarter)
        return pair_stack(pair_stack(part, "x", 1), "core", 1)

    def fetch_gate_up(weight):
        rows = weight.shape[0]
        split = blocks(weight.reshape(rows, 2, FF))
        f = split.shape[-1]
        mine = lax.dynamic_slice(
            split, (0, core, me_x * (outer // 2), 0, 0), (rows, 1, outer // 2, 4, f)
        )[:, 0]
        sent = jnp.moveaxis(mine, -2, 0).reshape(4, rows, -1)
        part = row_unblocks(outer_stack(square_exchange(sent)))
        return pair_stack(pair_stack(part, "x", 1), "core", 1)

    def finish(part, dim):
        mine = pair_stack(low(part), "x", dim)
        return pair_stack(mine, "core", dim).astype(F32)

    def two_cores(value):
        return jnp.concatenate([value, swap(value, "core")])

    def two_cores_half(value):
        half = value.shape[1] // 2
        sent = lax.dynamic_slice_in_dim(value, (1 - core) * half, half, 1)
        kept = lax.dynamic_slice_in_dim(value, core * half, half, 1)
        return jnp.concatenate([kept, swap(sent, "core")])

    def weight_grad(left_both, grad):
        both = two_cores_half(grad)
        return pair_reduce(dot(left_both, both, ((0,), (0,))).astype(LOW), "x", 1)

    cond_rows = ada_weight.shape[0]
    cond_low = lax.dynamic_slice_in_dim(jax.nn.silu(condition), me_b * cond_rows, cond_rows, 1).astype(LOW)
    mod_sum = group_sum(dot(cond_low, ada_weight))
    modulation = mod_sum + ada_bias
    cond_all = all_dp(cond_low).reshape(-1, cond_rows)

    ints = jnp.concatenate([segments[None], positions]).T
    ints = gather_square(ints)
    seg_square, pos_square = ints[:, 0], ints[:, 1:].T
    seg_far = far(seg_square[None])
    seg_col, seg_row = seg_square[:, None], seg_square[None]

    source = hidden.astype(F32)
    hidden_square = gather_square(hidden).astype(F32)
    qkv_mine = fetch_qkv(qkv_weight)

    chosen = jnp.where(dropped[:, None, None] == 1, null_caption[None], captions)
    chosen_rows = chosen.reshape(CLIPS * CAP, chosen.shape[2])
    caption_part = dot(chosen_rows, caption_weight)
    split = blocks(caption_part.reshape(CLIPS * CAP, 2, D))
    split = jnp.moveaxis(split, -2, 0).reshape(4 * CLIPS * CAP, -1)

    def scatter_place(full):
        count = full.shape[0] // 4
        parts = [lax.dynamic_slice_in_dim(full, (me_c ^ r) * count, count, 0) for r in range(4)]
        return scatter_square(jnp.concatenate(parts))

    caption_mine = outer_sum(scatter_place(split))

    outw = fetch_rows(out_weight)
    gate_up_mine = fetch_gate_up(gate_up)
    down_mine = fetch_rows(down_weight)

    first_clip = seg_square[:, None] == 0

    def per_token(rows, sel):
        return jnp.where(sel, rows[0:1], rows[1:2])

    scale_square = per_token(modulation[:, :D], first_clip)
    first_in = (unit_rows(hidden_square) * gains[0] * (1.0 + scale_square)).astype(LOW)
    projected = dot(first_in, qkv_mine)
    q_raw, k_raw, v_raw = projected[:, :width], projected[:, width : 2 * width], projected[:, 2 * width :]
    ck_raw = caption_mine[:, :width]
    sums, sums_c = square_sum(
        jnp.stack([jnp.sum(q_raw * q_raw, -1), jnp.sum(k_raw * k_raw, -1)]), jnp.sum(ck_raw * ck_raw, -1)
    )
    inv = lax.rsqrt(sums / D + EPSILON)[:, :, None]
    inv_q, inv_k = inv[0], inv[1]
    inv_c = lax.rsqrt(sums_c / D + EPSILON)[:, None]
    gain_q, gain_k, gain_c = (my_cols(gains[i])[None] for i in (4, 5, 6))

    pair_index = jnp.arange(HEAD) // 2
    frequency = 10000.0 ** (-3.0 * (pair_index // 3).astype(F32) / (HEAD // 2))
    select = ((pair_index % 3)[None, :] == jnp.arange(3)[:, None]).astype(F32)
    angles = jnp.dot(pos_square.astype(F32).T, select, precision=PRECISE) * frequency[None, :]
    cosine = jnp.tile(jnp.cos(angles), (1, width // HEAD))
    sine = jnp.tile(jnp.sin(angles), (1, width // HEAD))
    lane = jnp.arange(width)
    turn = jnp.where(
        (lane[:, None] ^ 1) == lane[None, :], jnp.where(lane[None, :] % 2 == 0, -1.0, 1.0), 0.0
    ).astype(F32)

    def rotate(values, sign):
        return values * cosine + jnp.dot(values, turn, precision=PRECISE) * (sign * sine)

    unit_q, unit_k = q_raw * inv_q, k_raw * inv_k
    scaling = HEAD**-0.5
    queries = rotate(unit_q * gain_q, 1.0).astype(LOW) * jnp.asarray(scaling, LOW)
    keys = rotate(unit_k * gain_k, 1.0).astype(LOW)
    values = v_raw.astype(LOW)
    unit_c = ck_raw * inv_c
    cap_keys = (unit_c * gain_c).astype(LOW)
    cap_values = caption_mine[:, width:].astype(LOW)
    keys_far, values_far = far(keys), far(values)

    near, away, back_away, back_near = attention_calls(square, width, CLIPS * CAP, outer - 1)
    out_near, out_cross, stats = near(queries, keys, values, cap_keys, cap_values, seg_col, seg_row)
    head_tanh = jnp.tanh(head_gate)
    gate_row = my_cols(jnp.repeat(head_tanh, HEAD))[None]
    out_self, mixed, lse = away(
        queries, keys_far, values_far, seg_col, seg_far, out_near, out_cross, stats, gate_row
    )
    mixed_both = two_cores(mixed)
    attended = scatter_square(dot(mixed, outw))

    clip_here = segments[:, None] == 0
    gate_attn = jnp.tanh(per_token(modulation[:, D : 2 * D], clip_here))
    scale_ffn = per_token(modulation[:, 2 * D : 3 * D], clip_here)
    gate_ffn = jnp.tanh(per_token(modulation[:, 3 * D :], clip_here))
    attn_unit = unit_rows(attended)
    middle = source + gate_attn * attn_unit * gains[1]
    unit_mid = unit_rows(middle)
    second_low = (unit_mid * gains[2] * (1.0 + scale_ffn)).astype(LOW)
    second_in = gather_square(second_low)
    second_both = two_cores(second_in)
    hidden_units = FF // 4
    gate_values = dot(second_in, gate_up_mine)
    gate_part, up_part = gate_values[:, :hidden_units], gate_values[:, hidden_units:]
    activated = (jax.nn.silu(gate_part) * up_part).astype(LOW)
    activated_both = two_cores(activated)
    lowered = scatter_square(dot(activated, down_mine))
    low_unit = unit_rows(lowered)
    result = middle + gate_ffn * low_unit * gains[3]

    upstream = cotangent.astype(F32)
    d_gate_ffn = upstream * low_unit * gains[3] * (1.0 - gate_ffn * gate_ffn)
    d_lowered, grad_gain3 = norm_back(upstream * gate_ffn, lowered, gains[3])
    d_lowered_sq = gather_square(d_lowered.astype(LOW))
    d_activated = dot(d_lowered_sq, down_mine, ((1,), (1,)))
    sigmoid = jax.nn.sigmoid(gate_part)
    d_gate_part = d_activated * up_part * sigmoid * (1.0 + gate_part * (1.0 - sigmoid))
    d_up_part = d_activated * gate_part * sigmoid
    d_gate_values = jnp.concatenate([d_gate_part, d_up_part], 1).astype(LOW)
    d_second = scatter_square(dot(d_gate_values, gate_up_mine, ((1,), (1,))))

    down_part = weight_grad(activated_both, d_lowered_sq)
    grad_down = finish(outer_reduce(down_part.reshape(outer, -1, D // 4)), 1)
    up_quarter = weight_grad(second_both, d_gate_values)
    up_quarter = outer_reduce(row_blocks(up_quarter))
    up_quarter = square_exchange(low(up_quarter))
    rows_up = gate_up.shape[0]
    half_outer = outer // 2
    up_quarter = up_quarter.reshape(4, rows_up, half_outer, -1).transpose(1, 2, 0, 3)

    def finish_gate_up(part):
        if not lead:
            return finish(part.reshape(rows_up, -1).astype(F32), 1)
        whole = finish(part.astype(F32)[:, None], 1)
        whole = whole.reshape(rows_up, 2, outer, 4, -1)
        return unblocks(whole).reshape(rows_up, -1)

    grad_gate_up = finish_gate_up(up_quarter)

    d_scale_ffn = d_second * unit_mid * gains[2]
    d_middle_norm, grad_gain2 = norm_back(d_second * (1.0 + scale_ffn), middle, gains[2])
    d_middle = upstream + d_middle_norm
    d_gate_attn = d_middle * attn_unit * gains[1] * (1.0 - gate_attn * gate_attn)
    d_attended, grad_gain1 = norm_back(d_middle * gate_attn, attended, gains[1])

    d_attended_sq = gather_square(d_attended.astype(LOW))
    d_mixed = dot(d_attended_sq, outw, ((1,), (1,))).astype(LOW)
    dq_part, dk_far, dv_far, dck, dcv, d_head, delta = back_away(
        queries, d_mixed, out_self, out_cross, lse, stats, gate_row, keys_far, values_far, cap_keys, cap_values,
        seg_col, seg_far,
    )
    dk_other, dv_other = far_back(dk_far), far_back(dv_far)
    d_query, dk_near, dv_near = back_near(
        queries, d_mixed, lse, delta, keys, values, seg_col, seg_row, dq_part
    )
    d_cap = outer_sum(jnp.concatenate([dck, dcv], 1))
    d_key, d_value = dk_near + dk_other, dv_near + dv_other

    out_part = weight_grad(mixed_both, d_attended_sq)
    grad_out = finish(outer_reduce(out_part.reshape(outer, -1, D // 4)), 1)

    turned_q, turned_k = rotate(d_query, -1.0), rotate(d_key, -1.0)
    inner_q, inner_k = turned_q * gain_q, turned_k * gain_k
    inner_c = d_cap[:, :width] * gain_c
    sums, sums_c = square_sum(
        jnp.stack([jnp.sum(inner_q * unit_q, -1), jnp.sum(inner_k * unit_k, -1)]), jnp.sum(inner_c * unit_c, -1)
    )
    mean = (sums / D)[:, :, None]
    d_q_raw = inv_q * (inner_q - unit_q * mean[0])
    d_k_raw = inv_k * (inner_k - unit_k * mean[1])
    d_c_raw = inv_c * (inner_c - unit_c * (sums_c / D)[:, None])
    d_projected = jnp.concatenate([d_q_raw, d_k_raw, d_value], 1).astype(LOW)
    d_first = scatter_square(dot(d_projected, qkv_mine, ((1,), (1,))))

    rows_qkv = qkv_weight.shape[0]
    quarter = rows_qkv // 4
    qkv_part = low(dot(first_in, d_projected, ((0,), (0,))))
    qkv_part = row_blocks(qkv_part).reshape(outer, 4, 2, 2, quarter, -1)
    qkv_part = pair_reduce(qkv_part, "core", 2)[:, :, 0]
    qkv_part = pair_reduce(qkv_part, "x", 2)[:, :, 0]
    qkv_part = square_exchange(low(outer_reduce(qkv_part)))
    qkv_part = qkv_part.reshape(4, quarter, 3, outer, -1).transpose(1, 2, 3, 0, 4)
    qkv_part = unblocks(qkv_part).reshape(quarter, -1)
    grad_qkv = finish(qkv_part.astype(F32), 0)

    d_cap_mine = jnp.concatenate([d_c_raw, d_cap[:, width:]], 1).astype(LOW)

    def gather_place(value):
        full = gather_square(value)
        count = value.shape[0]
        result = jnp.zeros((4,) + value.shape, value.dtype)
        for r in range(4):
            result = lax.dynamic_update_slice_in_dim(result, full[None, r * count : (r + 1) * count], me_c ^ r, 0)
        return result

    d_cap_all = gather_place(d_cap_mine).reshape(4, CLIPS * CAP, 2, outer, -1)
    d_cap_low = unblocks(jnp.moveaxis(d_cap_all, 0, -2)).reshape(CLIPS * CAP, 2 * D)
    grad_caption = finish(weight_grad(two_cores(chosen_rows), d_cap_low), 1)
    d_chosen = dot(d_cap_low, caption_weight, ((1,), (1,))).reshape(CLIPS, CAP, -1)
    grad_null = jnp.sum(jnp.where(dropped[:, None, None] == 1, d_chosen, 0.0), 0)
    grad_null = rounded(grad_null) + swap(low(grad_null), "core").astype(F32)
    grad_null = rounded(grad_null) + swap(low(grad_null), "x").astype(F32)

    scale_attn = per_token(modulation[:, :D], clip_here)
    unit_in = unit_rows(source)
    d_scale_attn = d_first * unit_in * gains[0]
    d_source_norm, grad_gain0 = norm_back(d_first * (1.0 + scale_attn), source, gains[0])
    input_grad = d_middle + d_source_norm

    onehot = (segments[:, None] == jnp.arange(CLIPS)[None, :]).astype(F32)

    def per_clip(grad):
        return lax.dot_general(onehot, grad, (((0,), (0,)), ((), ())), precision=PRECISE)

    early = jnp.concatenate(
        [per_clip(d_gate_attn), per_clip(d_scale_ffn), per_clip(d_gate_ffn), grad_gain1[None], grad_gain2[None], grad_gain3[None]]
    )
    grad_gain6 = jnp.where(me_o == 0, jnp.sum(d_cap[:, :width] * unit_c, 0), 0.0)
    late = jnp.concatenate(
        [
            per_clip(d_scale_attn),
            grad_gain0[None],
            put_cols(jnp.sum(turned_q * unit_q, 0))[None],
            put_cols(jnp.sum(turned_k * unit_k, 0))[None],
            put_cols(grad_gain6)[None],
            put_cols(d_head[0])[None],
        ]
    )
    early = all_dp(low(group_sum(early))).astype(F32)
    late = all_dp(low(group_sum(late))).astype(F32)
    d_mod = jnp.concatenate([late[:, :, 0:2], early[:, :, 0:2], early[:, :, 2:4], early[:, :, 4:6]], -1)
    d_mod = d_mod.reshape(4 * CLIPS, 4 * D)
    grad_ada = dot(cond_all, d_mod.astype(LOW), ((0,), (0,)))
    grad_ada_b = jnp.sum(d_mod, 0)
    early_sum, late_sum = jnp.sum(early[:, :, 6:], (0, 1)), jnp.sum(late[:, :, 2:], (0, 1))
    grad_gains = jnp.concatenate([late_sum[0:1], early_sum, late_sum[1:4]])
    grad_head = jnp.sum(late_sum[4].reshape(HEADS, HEAD), -1) * (1.0 - head_tanh * head_tanh)
    return (
        result,
        input_grad,
        grad_ada,
        grad_ada_b,
        grad_qkv,
        grad_out,
        grad_caption,
        grad_gate_up,
        grad_down,
        grad_null,
        grad_gains,
        grad_head,
    )


def solution(mesh):
    devices = mesh.devices
    outer = devices.shape[1] // 4
    lead = (D // devices.shape[1]) % HEAD != 0
    if lead:
        grid = Mesh(devices.reshape(2, 2, 2, 2, outer), ("x", "core", "p", "y", "o"))
        blk = ("p", "y", "o")
    else:
        grid = Mesh(devices.reshape(2, 2, outer, 2, 2), ("x", "core", "o", "p", "y"))
        blk = ("o", "p", "y")
    dp = ("x", "core")
    every = dp + blk
    in_specs = (
        P(every, None),
        P(every),
        P(None, every),
        P(dp, None),
        P(dp, None, blk),
        P(dp),
        P(None, blk),
        P(blk, None),
        P(),
        P(blk, None),
        P(blk, None),
        P(blk, None),
        P(blk, None),
        P(blk, None),
        P(),
        P(),
        P(every, None),
    )
    out_specs = (
        P(every, None),
        P(every, None),
        P(blk, None),
        P(),
        P(blk, None),
        P(blk, None),
        P(blk, None),
        P(blk, None),
        P(blk, None),
        P(None, blk),
        P(),
        P(),
    )
    return jax.shard_map(
        functools.partial(on_device, outer, lead),
        mesh=grid,
        in_specs=in_specs,
        out_specs=out_specs,
        check_vma=False,
    )
```

```python
import functools

import jax
import jax.numpy as jnp
from jax import lax
from jax.experimental import pallas as pl
from jax.experimental.pallas import tpu as pltpu
from jax.sharding import Mesh, PartitionSpec as P

HEADS = 24
HEAD = 64
D = 1536
FF = 4096
CAP = 128
CLIPS = 2
PAIR = 2 * HEAD

PRECISE = lax.Precision.HIGHEST
EPSILON = 1e-06
NEGATIVE = -1e30
F32 = jnp.float32
LOW = jnp.bfloat16
SWAP = [(0, 1), (1, 0)]


def inv_root(values):
    return lax.rsqrt(jnp.mean(values * values, -1, keepdims=True) + EPSILON)


def unit_rows(values):
    return values * inv_root(values)


def norm_back(grad_in, values, gain):
    root = inv_root(values)
    normed = values * root
    inner = grad_in * gain
    back = root * (inner - normed * jnp.mean(inner * normed, -1, keepdims=True))
    return back, jnp.sum(grad_in * normed, 0)


def rounded(values):
    return lax.reduce_precision(values, 8, 7)


def low(values):
    return rounded(values).astype(LOW)


def dot(a, b, dims=((1,), (0,))):
    return lax.dot_general(a, b, (dims, ((), ())), preferred_element_type=F32)


def nt(a, b):
    return lax.dot_general(a, b, (((1,), (1,)), ((), ())), preferred_element_type=F32)


def tn(a, b):
    return lax.dot_general(a, b, (((0,), (0,)), ((), ())), preferred_element_type=F32)


def nn(a, b):
    return lax.dot_general(a, b, (((1,), (0,)), ((), ())), preferred_element_type=F32)


def cross_bias(seg_col, count):
    clip = lax.broadcasted_iota(jnp.int32, (1, count), 1) // CAP
    return jnp.where(seg_col == clip, 0.0, NEGATIVE)


def forward_near(q_ref, k_ref, v_ref, ck_ref, cv_ref, sq_ref, sk_ref, o_ref, oc_ref, st_ref):
    seg_col = sq_ref[...]
    bias = jnp.where(seg_col == sk_ref[...], 0.0, NEGATIVE)
    bias_cross = cross_bias(seg_col, ck_ref.shape[0])
    for h in range(2):
        at = slice(h * HEAD, (h + 1) * HEAD)
        q = q_ref[:, at]
        s = nt(q, k_ref[:, at]) + bias
        m = jnp.max(s, -1, keepdims=True)
        e = jnp.exp(s - m)
        st_ref[0, :, h : h + 1] = m
        st_ref[0, :, 2 + h : 3 + h] = jnp.sum(e, -1, keepdims=True)
        o_ref[:, at] = nn(e.astype(LOW), v_ref[:, at])
        s = nt(q, ck_ref[:, at]) + bias_cross
        m = jnp.max(s, -1, keepdims=True)
        e = jnp.exp(s - m)
        total = jnp.sum(e, -1, keepdims=True)
        st_ref[0, :, 4 + h : 5 + h] = m + jnp.log(total)
        oc_ref[:, at] = nn(e.astype(LOW), cv_ref[:, at]) / total


def forward_far(
    count, q_ref, k_ref, v_ref, sq_ref, sk_ref, o_ref, oc_ref, st_ref, gate_ref, os_ref, mix_ref, lse_ref, m_ref, l_ref
):
    step = pl.program_id(1)

    @pl.when(step == 0)
    def _():
        os_ref[...] = o_ref[...]
        m_ref[...] = st_ref[0, :, 0:2]
        l_ref[...] = st_ref[0, :, 2:4]

    bias = jnp.where(sq_ref[...] == sk_ref[0], 0.0, NEGATIVE)
    for h in range(2):
        at = slice(h * HEAD, (h + 1) * HEAD)
        s = nt(q_ref[:, at], k_ref[0, :, at]) + bias
        before = m_ref[:, h : h + 1]
        m = jnp.maximum(before, jnp.max(s, -1, keepdims=True))
        e = jnp.exp(s - m)
        factor = jnp.exp(before - m)
        m_ref[:, h : h + 1] = m
        l_ref[:, h : h + 1] = l_ref[:, h : h + 1] * factor + jnp.sum(e, -1, keepdims=True)
        os_ref[:, at] = os_ref[:, at] * factor + nn(e.astype(LOW), v_ref[0, :, at])

    @pl.when(step == count - 1)
    def _():
        for h in range(2):
            at = slice(h * HEAD, (h + 1) * HEAD)
            total = l_ref[:, h : h + 1]
            out = os_ref[:, at] / total
            os_ref[:, at] = out
            mix_ref[:, at] = (out + gate_ref[:, at] * oc_ref[:, at]).astype(LOW)
            lse_ref[0, :, h : h + 1] = m_ref[:, h : h + 1] + jnp.log(total)


def backward_far(
    q_ref, g_ref, os_ref, oc_ref, lse_ref, st_ref, gate_ref, k_ref, v_ref, ck_ref, cv_ref, sq_ref, sk_ref,
    dq_ref, dkv_ref, dck_ref, dcv_ref, dh_ref, delta_ref,
):
    step = pl.program_id(1)
    seg_col = sq_ref[...]
    scaling = HEAD**-0.5

    @pl.when(step == 0)
    def _():
        bias_cross = cross_bias(seg_col, ck_ref.shape[0])
        g = g_ref[...].astype(F32)
        dh_ref[...] = jnp.sum(g * oc_ref[...], 0, keepdims=True)
        for h in range(2):
            at = slice(h * HEAD, (h + 1) * HEAD)
            gh = g[:, at]
            delta_ref[0, :, h : h + 1] = jnp.sum(gh * os_ref[:, at], -1, keepdims=True)
            gc = (gate_ref[:, at] * gh).astype(LOW)
            delta = jnp.sum(gc.astype(F32) * oc_ref[:, at], -1, keepdims=True)
            q = q_ref[:, at]
            p = jnp.exp(nt(q, ck_ref[:, at]) + bias_cross - st_ref[0, :, 4 + h : 5 + h])
            ds = (p * (nt(gc, cv_ref[:, at]) - delta)).astype(LOW)
            dq_ref[:, at] = nn(ds, ck_ref[:, at]) * scaling
            dck_ref[:, at] = tn(ds, q).astype(dck_ref.dtype)
            dcv_ref[:, at] = tn(p.astype(LOW), gc).astype(dcv_ref.dtype)

    bias = jnp.where(seg_col == sk_ref[0], 0.0, NEGATIVE)
    for h in range(2):
        at = slice(h * HEAD, (h + 1) * HEAD)
        q = q_ref[:, at]
        g = g_ref[:, at]
        k = k_ref[0, :, at]
        p = jnp.exp(nt(q, k) + bias - lse_ref[0, :, h : h + 1])
        ds = (p * (nt(g, v_ref[0, :, at]) - delta_ref[0, :, h : h + 1])).astype(LOW)
        dq_ref[:, at] += nn(ds, k) * scaling
        dkv_ref[0, 0, :, at] = tn(ds, q).astype(LOW)
        dkv_ref[0, 1, :, at] = tn(p.astype(LOW), g).astype(LOW)


def backward_near(q_ref, g_ref, lse_ref, delta_ref, k_ref, v_ref, sq_ref, sk_ref, dp_ref, dq_ref, dk_ref, dv_ref):
    bias = jnp.where(sq_ref[...] == sk_ref[...], 0.0, NEGATIVE)
    scaling = HEAD**-0.5
    for h in range(2):
        at = slice(h * HEAD, (h + 1) * HEAD)
        q = q_ref[:, at]
        g = g_ref[:, at]
        k = k_ref[:, at]
        p = jnp.exp(nt(q, k) + bias - lse_ref[0, :, h : h + 1])
        ds = (p * (nt(g, v_ref[:, at]) - delta_ref[0, :, h : h + 1])).astype(LOW)
        dq_ref[:, at] = dp_ref[:, at] + nn(ds, k) * scaling
        dk_ref[:, at] = tn(ds, q)
        dv_ref[:, at] = tn(p.astype(LOW), g)


def swapped(x):
    lane = lax.broadcasted_iota(jnp.int32, x.shape, 1)
    return jnp.where(lane % 2 == 0, pltpu.roll(x, x.shape[1] - 1, 1), pltpu.roll(x, 1, 1))


def heads_in(q_ref, k_ref, v_ref, inv_ref, gq_ref, gk_ref, cos_ref, sin_ref, q_out, kv_out):
    cosine, sine = cos_ref[...], sin_ref[...]
    q = q_ref[...] * inv_ref[:, 0:1] * gq_ref[...]
    k = k_ref[...] * inv_ref[:, 1:2] * gk_ref[...]
    q = (q * cosine + swapped(q) * sine).astype(LOW)
    q_out[...] = (q.astype(F32) * HEAD**-0.5).astype(LOW)
    kv_out[0] = (k * cosine + swapped(k) * sine).astype(LOW)
    kv_out[1] = v_ref[...].astype(LOW)


def heads_back(
    dq_ref, dk_ref, far_ref, q_ref, k_ref, inv_ref, gq_ref, gk_ref, cos_ref, sin_ref, iq_out, ik_out, st_out, gg_out
):
    cosine, sine = cos_ref[...], sin_ref[...]
    dq = dq_ref[...]
    dk = dk_ref[...] + far_ref[0].astype(F32)
    uq = q_ref[...] * inv_ref[:, 0:1]
    uk = k_ref[...] * inv_ref[:, 1:2]
    tq = dq * cosine - swapped(dq) * sine
    tk = dk * cosine - swapped(dk) * sine
    gg_out[0:1] = jnp.sum(tq * uq, 0, keepdims=True)
    gg_out[1:2] = jnp.sum(tk * uk, 0, keepdims=True)
    iq = tq * gq_ref[...]
    ik = tk * gk_ref[...]
    iq_out[...] = iq
    ik_out[...] = ik
    st_out[0, :, 0:1] = jnp.sum(iq * uq, -1, keepdims=True)
    st_out[0, :, 1:2] = jnp.sum(ik * uk, -1, keepdims=True)


def head_calls(tokens, width):
    pairs = width // PAIR
    sds = jax.ShapeDtypeStruct

    def at(first):
        return pl.BlockSpec((tokens, PAIR), lambda i: (0, first + i))

    row = pl.BlockSpec((1, PAIR), lambda i: (0, i))
    fixed = pl.BlockSpec((tokens, PAIR), lambda i: (0, 0))
    inv = pl.BlockSpec((tokens, 2), lambda i: (0, 0))
    both = pl.BlockSpec((2, tokens, PAIR), lambda i: (0, 0, i))
    cost = pl.CostEstimate(flops=20 * tokens * width, bytes_accessed=20 * tokens * width, transcendentals=0)
    into = pl.pallas_call(
        heads_in,
        grid=(pairs,),
        in_specs=[at(0), at(pairs), at(2 * pairs), inv, row, row, fixed, fixed],
        out_specs=[at(0), both],
        out_shape=[sds((tokens, width), LOW), sds((2, tokens, width), LOW)],
        cost_estimate=cost,
        name="heads_in",
    )
    back = pl.pallas_call(
        heads_back,
        grid=(pairs,),
        in_specs=[at(0), at(0), pl.BlockSpec((1, tokens, PAIR), lambda i: (0, 0, i)), at(0), at(pairs), inv, row, row, fixed, fixed],
        out_specs=[at(0), at(0), pl.BlockSpec((1, tokens, 2), lambda i: (i, 0, 0)), pl.BlockSpec((2, PAIR), lambda i: (0, i))],
        out_shape=[sds((tokens, width), F32), sds((tokens, width), F32), sds((pairs, tokens, 2), F32), sds((2, width), F32)],
        cost_estimate=cost,
        name="heads_back",
    )
    return into, back


def place_columns(place, groups, outer, rest, lead):
    whole = 4 * outer * rest
    return [
        g * whole + ((place * outer + o) if lead else (o * 4 + place)) * rest for g in range(groups) for o in range(outer)
    ]


def cut_kernel(columns, rest, me_ref, x_ref, *outs):
    for me in range(4):

        @pl.when(me_ref[0] == me)
        def _():
            for r, out in enumerate(outs):
                for j, start in enumerate(columns[me ^ r]):
                    out[:, j * rest : (j + 1) * rest] = x_ref[:, start : start + rest]


def lay_kernel(columns, rest, blank, me_ref, *refs):
    ins, out = refs[:-1], refs[-1]
    if blank:
        out[...] = jnp.zeros_like(out)
    for me in range(4):

        @pl.when(me_ref[0] == me)
        def _():
            for r, value in enumerate(ins):
                for j, start in enumerate(columns[me ^ r]):
                    out[:, start : start + rest] = value[:, j * rest : (j + 1) * rest]


def caption_kernel(columns, rest, rows_ref, weight_ref, out_ref):
    product = nn(rows_ref[...], weight_ref[...])
    for place in range(4):
        for j, start in enumerate(columns[place]):
            out_ref[place, :, j * rest : (j + 1) * rest] = product[:, start : start + rest].astype(out_ref.dtype)


def assemble_kernel(plan, width, at_ref, *refs):
    ins, out, sems = refs[:-2], refs[-2], refs[-1]
    copies = []
    for i, (source, first, rows) in enumerate(plan):
        row = pl.multiple_of(at_ref[2 * i], 16)
        col = pl.multiple_of(at_ref[2 * i + 1], 128)
        copies.append(
            pltpu.make_async_copy(
                ins[source].at[pl.ds(first, rows)], out.at[pl.ds(row, rows), pl.ds(col, width)], sems.at[i]
            )
        )
    for copy in copies:
        copy.start()
    for copy in copies:
        copy.wait()


def product_kernel(left_ref, right_ref, out_ref):
    out_ref[0] = tn(left_ref[...], right_ref[...]).astype(out_ref.dtype)


def grad_product(left, right, parts):
    rows, cols = left.shape[1], right.shape[1] // parts
    tile = 512 if rows % 512 == 0 else rows
    return pl.pallas_call(
        product_kernel,
        grid=(parts, rows // tile),
        in_specs=[
            pl.BlockSpec((left.shape[0], tile), lambda q, i: (0, i)),
            pl.BlockSpec((left.shape[0], cols), lambda q, i: (0, q)),
        ],
        out_specs=pl.BlockSpec((1, tile, cols), lambda q, i: (q, i, 0)),
        out_shape=jax.ShapeDtypeStruct((parts, rows, cols), LOW),
        cost_estimate=pl.CostEstimate(
            flops=2 * left.shape[0] * rows * right.shape[1],
            bytes_accessed=2 * (rows * right.shape[1] + left.size + right.size),
            transcendentals=0,
        ),
        compiler_params=pltpu.CompilerParams(fuse_transposed_lhs_in_matmul=True),
        name="grad_product",
    )(left, right)


def assemble(inputs, plan, places, shape):
    width = inputs[0].shape[1]
    at = jnp.stack([jnp.asarray(v, jnp.int32) for pair in places for v in pair])
    size = 2 * shape[0] * shape[1] * 2
    return pl.pallas_call(
        functools.partial(assemble_kernel, plan, width),
        grid_spec=pltpu.PrefetchScalarGridSpec(
            num_scalar_prefetch=1,
            grid=(1,),
            in_specs=[pl.BlockSpec(memory_space=pl.ANY)] * len(inputs),
            out_specs=pl.BlockSpec(memory_space=pltpu.VMEM),
            scratch_shapes=[pltpu.SemaphoreType.DMA((len(plan),))],
        ),
        out_shape=jax.ShapeDtypeStruct(shape, inputs[0].dtype),
        compiler_params=pltpu.CompilerParams(vmem_limit_bytes=32 * 1024 * 1024),
        cost_estimate=pl.CostEstimate(flops=0, bytes_accessed=size, transcendentals=0),
        name="assemble",
    )(at, *inputs)


def attention_calls(tokens, width, capt, far):
    pairs = width // PAIR
    sds = jax.ShapeDtypeStruct

    def cols(rows):
        return pl.BlockSpec((rows, PAIR), lambda i, *r: (0, i))

    def stat(n):
        return pl.BlockSpec((1, tokens, n), lambda i, *r: (i, 0, 0))

    seg_col = pl.BlockSpec((tokens, 1), lambda i, *r: (0, 0))
    seg_row = pl.BlockSpec((1, tokens), lambda i, *r: (0, 0))
    far_k = pl.BlockSpec((1, None, tokens, PAIR), lambda i, r: (r, 0, 0, i))
    far_v = pl.BlockSpec((1, None, tokens, PAIR), lambda i, r: (r, 1, 0, i))
    far_both = pl.BlockSpec((1, 2, tokens, PAIR), lambda i, r: (r, 0, 0, i))
    near_k = pl.BlockSpec((None, tokens, PAIR), lambda i, *r: (0, 0, i))
    near_v = pl.BlockSpec((None, tokens, PAIR), lambda i, *r: (1, 0, i))
    far_row = pl.BlockSpec((1, 1, tokens), lambda i, r: (r, 0, 0))
    gate = cols(1)
    tok, cap = cols(tokens), cols(capt)

    def cost(keys, products):
        return pl.CostEstimate(
            flops=2 * tokens * keys * width * products,
            bytes_accessed=8 * tokens * width * 4,
            transcendentals=tokens * keys * (width // HEAD),
        )

    params = pltpu.CompilerParams(vmem_limit_bytes=48 * 1024 * 1024)
    near = pl.pallas_call(
        forward_near,
        grid=(pairs,),
        in_specs=[tok, near_k, near_v, cap, cap, seg_col, seg_row],
        out_specs=[tok, tok, stat(8)],
        out_shape=[sds((tokens, width), F32), sds((tokens, width), F32), sds((pairs, tokens, 8), F32)],
        compiler_params=params,
        cost_estimate=cost(tokens + capt, 2),
        name="attn_near",
    )
    away = pl.pallas_call(
        functools.partial(forward_far, far),
        grid=(pairs, far),
        in_specs=[tok, far_k, far_v, seg_col, far_row, tok, tok, stat(8), gate],
        out_specs=[tok, tok, stat(2)],
        out_shape=[sds((tokens, width), F32), sds((tokens, width), LOW), sds((pairs, tokens, 2), F32)],
        scratch_shapes=[pltpu.VMEM((tokens, 2), F32), pltpu.VMEM((tokens, 2), F32)],
        compiler_params=params,
        cost_estimate=cost(tokens * far, 2),
        name="attn_far",
    )
    back_away = pl.pallas_call(
        backward_far,
        grid=(pairs, far),
        in_specs=[tok, tok, tok, tok, stat(2), stat(8), gate, far_k, far_v, cap, cap, seg_col, far_row],
        out_specs=[tok, far_both, cap, cap, gate, stat(2)],
        out_shape=[
            sds((tokens, width), F32),
            sds((far, 2, tokens, width), LOW),
            sds((capt, width), F32),
            sds((capt, width), F32),
            sds((1, width), F32),
            sds((pairs, tokens, 2), F32),
        ],
        compiler_params=params,
        cost_estimate=cost(tokens * far + capt, 5),
        name="attn_back_far",
    )
    back_near = pl.pallas_call(
        backward_near,
        grid=(pairs,),
        in_specs=[tok, tok, stat(2), stat(2), near_k, near_v, seg_col, seg_row, tok],
        out_specs=[tok, tok, tok],
        out_shape=[sds((tokens, width), F32)] * 3,
        compiler_params=params,
        cost_estimate=cost(tokens, 5),
        name="attn_back_near",
    )
    return near, away, back_away, back_near


def swap(value, axis):
    return lax.ppermute(value, axis, SWAP)


def pair_stack(value, axis, dim):
    other = swap(value, axis)
    first = lax.axis_index(axis) == 0
    return jnp.concatenate([jnp.where(first, value, other), jnp.where(first, other, value)], dim)


def first_of(value):
    return value[(0,) * value.ndim].astype(F32)


def when(value):
    probe = first_of(value)
    return jnp.where(probe != probe, 1, 0)


def hold(value, *after):
    for other in after:
        value = value + (first_of(other) * 0.0).astype(value.dtype)
    return value


def on_device(
    outer,
    lead,
    hidden,
    segments,
    positions,
    condition,
    captions,
    dropped,
    null_caption,
    ada_weight,
    ada_bias,
    qkv_weight,
    out_weight,
    caption_weight,
    gate_up,
    down_weight,
    gains,
    head_gate,
    cotangent,
):
    me_c = lax.axis_index("p") * 2 + lax.axis_index("y")
    me_o = lax.axis_index("o")
    core = lax.axis_index("core")
    me_x = lax.axis_index("x")
    me_b = lax.axis_index(("p", "y", "o") if lead else ("o", "p", "y"))
    me_arg = me_c.reshape(1).astype(jnp.int32)
    tokens = hidden.shape[0]
    square = 4 * tokens
    width = D // 4
    capt = CLIPS * CAP
    blk = 4 * outer
    rest = D // blk
    mirrored = outer == 2
    t_axis, g_axis = ("core", "o") if mirrored else ("o", "core")
    t_size = 2 if mirrored else outer
    me_t, me_g = lax.axis_index(t_axis), lax.axis_index(g_axis)
    across = [[(i, i ^ r) for i in range(4)] for r in range(4)]
    beyond = [[(i, i ^ r) for i in range(outer)] for r in range(outer)]

    def unblocks(value):
        if lead:
            value = value.swapaxes(-3, -2)
        return value.reshape(value.shape[:-3] + (-1,))

    def row_blocks(value):
        size = value.shape[0] // blk
        if lead:
            return value.reshape((4, outer, size) + value.shape[1:]).swapaxes(0, 1)
        return value.reshape((outer, 4, size) + value.shape[1:])

    def block_index(o, c):
        return c * outer + o if lead else o * 4 + c

    def cut(value, groups, count):
        size = value.shape[1] // (groups * blk)
        columns = [place_columns(c, groups, outer, size, lead) for c in range(4)]
        out = jax.ShapeDtypeStruct((value.shape[0], groups * outer * size), value.dtype)
        return pl.pallas_call(
            functools.partial(cut_kernel, columns, size),
            in_specs=[pl.BlockSpec(memory_space=pltpu.SMEM), pl.BlockSpec(memory_space=pltpu.VMEM)],
            out_specs=[pl.BlockSpec(memory_space=pltpu.VMEM)] * count,
            out_shape=[out] * count,
            name="cut",
        )(me_arg, value)

    def lay(pieces, groups):
        size = pieces[0].shape[1] // (groups * outer)
        columns = [place_columns(c, groups, outer, size, lead) for c in range(4)]
        shape = (pieces[0].shape[0], 4 * pieces[0].shape[1])
        return pl.pallas_call(
            functools.partial(lay_kernel, columns, size, len(pieces) < 4),
            in_specs=[pl.BlockSpec(memory_space=pltpu.SMEM)] + [pl.BlockSpec(memory_space=pltpu.VMEM)] * len(pieces),
            out_specs=pl.BlockSpec(memory_space=pltpu.VMEM),
            out_shape=jax.ShapeDtypeStruct(shape, pieces[0].dtype),
            name="lay",
        )(me_arg, *pieces)

    def outer_reduce(value):
        if outer == 2:
            sent = lax.dynamic_index_in_dim(value, 1 - me_o, 0, keepdims=False).astype(LOW)
            kept = lax.dynamic_index_in_dim(value, me_o, 0, keepdims=False)
            return kept.astype(F32) + swap(sent, "o").astype(F32)
        return lax.psum_scatter(value.astype(LOW), "o", scatter_dimension=0).astype(F32)

    def axis_sum(value, axis):
        if axis != "o" or outer == 2:
            return rounded(value) + swap(low(value), axis).astype(F32)
        return lax.psum(low(value), axis).astype(F32)

    def mirror(value):
        if not mirrored:
            return value
        other = lax.ppermute(value, ("core", "o"), [(1, 2), (2, 1)])
        return jnp.where(core == me_o, value, other)

    def far(value):
        return jnp.stack([lax.ppermute(value, t_axis, [(i, i ^ r) for i in range(t_size)]) for r in range(1, t_size)])

    def to_place(value, r):
        return lax.ppermute(value, ("p", "y"), across[r])

    def gather_places(rows):
        return [rows] + [to_place(rows, r) for r in (1, 2, 3)]

    def gather_square(rows):
        return jnp.concatenate(gather_places(rows))

    def scatter_places(parts):
        total = parts[0]
        for r in (1, 2, 3):
            total = total + to_place(parts[r].astype(LOW), r).astype(F32)
        return total

    def scatter_square(full):
        return scatter_places([full[r * tokens : (r + 1) * tokens] for r in range(4)])

    def square_sum(value, shared=None):
        count = 4 * value.shape[0]
        whole = value.reshape(count, tokens)
        if shared is not None:
            whole = jnp.concatenate([whole, shared.reshape(-1, tokens)])
        for axis, order in (("y", (1, 0, 3, 2)), ("p", (2, 3, 0, 1))):
            other = swap(whole, axis)
            order = [4 * i + j for i in range(value.shape[0]) for j in order]
            whole = whole + jnp.concatenate([other[i : i + 1] for i in order] + [other[count:]])
        sums = whole[:count].reshape(value.shape)
        return sums if shared is None else (sums, whole[count:].reshape(-1))

    def sum_over(value, *axes):
        for axis in axes:
            value = axis_sum(value, axis)
        return value

    def hand_on(own, split, sent=None, later=(), last=()):
        pieces = [(own, 0, 0, 0)]
        if split:
            pieces += [(swap(own, "x"), 0, 1, 0)]
        for r in range(1, outer):
            far_piece = hold(lax.ppermute(own if sent is None else sent, "o", beyond[r]), *later)
            pieces += [(far_piece, 0, 0, r)]
            if split:
                pieces += [(hold(swap(far_piece, "x"), *last), 0, 1, r)]
        if split:
            pieces += [(swap(value, "core"), 1, x, o) for value, _, x, o in pieces]
        return pieces

    def fetch_qkv(weight, after):
        rows = weight.shape[0]
        split = (rows // 4) % 16 == 0
        quarter = rows // 4 if split else rows
        if split:
            weight = lax.dynamic_slice_in_dim(weight, (me_x * 2 + core) * quarter, quarter, 0)
        cuts = cut(weight, 3, 4)
        arrived = [to_place(cuts[r], r) for r in (1, 2, 3)]
        pieces = hand_on(hold(jnp.concatenate([cuts[0]] + arrived), after), split)
        plan, places = [], []
        for i, (_, k, x, o) in enumerate(pieces):
            for r in range(4):
                plan.append((i, r * quarter, quarter))
                at = block_index(me_o ^ o, me_c ^ r) * rows
                places.append((at + ((me_x ^ x) * 2 + (core ^ k)) * quarter if split else at, 0))
        whole = assemble([piece[0] for piece in pieces], plan, places, (D, 3 * D // 4))
        return whole, pieces, arrived

    def start_gate_up(weight, start):
        rows = weight.shape[0]
        f = FF // blk

        def piece_of(r):
            cols = []
            for j in range(outer // 2):
                o = me_x * (outer // 2) + j
                at = core * FF + block_index(o, me_c ^ r) * f + start
                cols.append(lax.dynamic_slice(weight, (0, at), (rows, f)))
            return jnp.concatenate(cols, 1) if len(cols) > 1 else cols[0]

        arrived = [to_place(piece_of(r), r) for r in (1, 2, 3)]
        own = jnp.concatenate([piece_of(0)] + arrived)
        return own, arrived

    def fetch_gate_up(own):
        rows, n = own.shape[0] // 4, own.shape[1]
        whole = lax.all_gather(own, ("core", "x", "o"), axis=0, tiled=True)
        plan, places = [], []
        for q in range(4):
            for o in range(outer):
                for r in range(4):
                    plan.append((0, ((q * outer + o) * 4 + r) * rows, rows))
                    places.append((block_index(o, me_c ^ r) * rows, q * n))
        return assemble([whole], plan, places, (D, 2 * FF // 4))

    def fetch_down(weight, after):
        rows, quarter = weight.shape[0], D // 4
        mine = lax.dynamic_slice(weight, (0, (core * 2 + me_x) * quarter), (rows, quarter))
        whole = lax.all_gather(hold(mine, after), ("core", "x", "o"), axis=0, tiled=True)
        plan = [(0, i * rows, rows) for i in range(4 * outer)]
        places = [(o * rows, q * quarter) for q in range(4) for o in range(outer)]
        return assemble([whole], plan, places, (outer * rows, D))

    def fetch_rows(weight, start, after, later):
        rows, quarter = weight.shape[0], D // 4
        mine = lax.dynamic_slice(weight, (0, (core * 2 + me_x) * quarter + start), (rows, quarter))
        pieces = hand_on(mine, True, hold(mine, *after), later)
        plan = [(i, 0, rows) for i in range(len(pieces))]
        places = [((me_o ^ o) * rows, ((core ^ k) * 2 + (me_x ^ x)) * quarter) for _, k, x, o in pieces]
        return assemble([piece[0] for piece in pieces], plan, places, (outer * rows, D)), pieces

    def finish(part, dim):
        return pair_stack(pair_stack(part, "x", dim), "core", dim).astype(F32)

    def two_cores(value):
        return jnp.concatenate([value, swap(value, "core")])

    def two_cores_half(value):
        half = value.shape[1] // 2
        first = core == 0
        a, b = value[:, :half], value[:, half:]
        return jnp.concatenate([jnp.where(first, a, b), swap(jnp.where(first, b, a), "core")])

    def grad_columns(left_both, grad_both):
        half = grad_both.shape[1] // 2
        theirs = lax.dynamic_slice_in_dim(grad_both, (1 - me_x) * half, half, 1)
        mine = lax.dynamic_slice_in_dim(grad_both, me_x * half, half, 1)
        sent = swap(dot(left_both, theirs, ((0,), (0,))).astype(LOW), "x")
        return dot(left_both, mine, ((0,), (0,))) + sent.astype(F32)

    numbers = jnp.concatenate([segments[None], positions]).T.astype(LOW)
    numbers = jnp.pad(numbers, ((0, 0), (0, 128 - numbers.shape[1])))
    mine = mirror(jnp.concatenate([hidden, numbers], 1))
    source = mine[:, :D].astype(F32)
    segment_here = mine[:, D].astype(jnp.int32)
    chosen = jnp.where(dropped[:, None, None] == 1, null_caption[None], captions)
    chosen_rows = chosen.reshape(capt, chosen.shape[2])
    caption_parts = pl.pallas_call(
        functools.partial(caption_kernel, [place_columns(c, 2, outer, rest, lead) for c in range(4)], rest),
        out_shape=jax.ShapeDtypeStruct((4, capt, 2 * width), LOW),
        in_specs=[pl.BlockSpec(memory_space=pltpu.VMEM)] * 2,
        out_specs=pl.BlockSpec(memory_space=pltpu.VMEM),
        compiler_params=pltpu.CompilerParams(vmem_limit_bytes=40 * 1024 * 1024),
        cost_estimate=pl.CostEstimate(
            flops=2 * capt * chosen_rows.shape[1] * 2 * D, bytes_accessed=8 * 1024 * 1024, transcendentals=0
        ),
        name="caption_product",
    )(chosen_rows, caption_weight)
    caption_parts = [lax.dynamic_index_in_dim(caption_parts, me_c ^ r, 0, keepdims=False) for r in range(4)]
    caption_half = scatter_places([caption_parts[0].astype(F32)] + caption_parts[1:])

    qkv_mine, qkv_pieces, qkv_arrived = fetch_qkv(qkv_weight, caption_half)
    tokens_blocks = gather_places(hold(mine, qkv_arrived[2], caption_half))
    tokens_square = jnp.concatenate(tokens_blocks)
    hidden_square = tokens_square[:, :D].astype(F32)
    seg_square = tokens_square[:, D].astype(jnp.int32)
    pos_square = tokens_square[:, D + 1 : D + 4].astype(F32)
    seg_col, seg_row = seg_square[:, None], seg_square[None]
    seg_far = far(seg_row)

    qkv_here = qkv_pieces[2][0] if outer == 2 else qkv_pieces[-1][0]
    late = when(qkv_here)

    cond_rows = ada_weight.shape[0]
    cond_low = lax.dynamic_slice_in_dim(jax.nn.silu(condition), me_b * cond_rows, cond_rows, 1).astype(LOW)
    cond_both = pair_stack(cond_low, "core", 0)
    cond_all = pair_stack(cond_both.reshape(2, 1, CLIPS, cond_rows), "x", 1).reshape(-1, cond_rows)
    modulation = sum_over(hold(dot(cond_both, ada_weight), qkv_here), "o", "y", "p")
    modulation = lax.dynamic_slice_in_dim(modulation, me_g * CLIPS, CLIPS, 0) + ada_bias

    up_own, up_arrived = start_gate_up(gate_up, when(tokens_blocks[3]))
    up_own = hold(up_own, qkv_here)


    head_tanh = jnp.tanh(head_gate)
    (place_gains,) = cut(jnp.concatenate([gains[4:7], jnp.repeat(head_tanh, HEAD)[None]]), 1, 1)
    gain_q, gain_k, gain_c, gate_row = (place_gains[i : i + 1] for i in range(4))

    pair_index = jnp.arange(PAIR) % HEAD // 2
    frequency = 10000.0 ** (-3.0 * (pair_index // 3).astype(F32) / (HEAD // 2))
    select = ((pair_index % 3)[None, :] == jnp.arange(3)[:, None]).astype(F32)
    angles = jnp.dot(pos_square, select, precision=PRECISE) * frequency[None, :]
    cosine = jnp.cos(angles)
    sine = jnp.sin(angles) * jnp.where(jnp.arange(PAIR) % 2 == 0, -1.0, 1.0)[None]

    def per_token(rows, sel):
        return jnp.where(sel, rows[0:1], rows[1:2])

    caption_mine = axis_sum(mirror(hold(caption_half, qkv_here).astype(LOW)).astype(F32), t_axis)
    scale_square = per_token(hold(modulation[:, :D], up_arrived[2], caption_mine, cosine), seg_col == 0)
    first_in = (unit_rows(hidden_square) * gains[0] * (1.0 + scale_square)).astype(LOW)
    projected = dot(first_in, qkv_mine)
    q_raw, k_raw = projected[:, :width], projected[:, width : 2 * width]
    ck_raw = caption_mine[:, :width]
    sums, sums_c = square_sum(
        jnp.stack([jnp.sum(q_raw * q_raw, -1), jnp.sum(k_raw * k_raw, -1)]), jnp.sum(ck_raw * ck_raw, -1)
    )
    outw, out_pieces = fetch_rows(out_weight, late, (), ())
    gate_up_mine = fetch_gate_up(up_own)
    down_mine = fetch_down(down_weight, projected)
    inv = hold(lax.rsqrt(sums / D + EPSILON).T, seg_far, out_pieces[2][0])
    heads_into, heads_out = head_calls(square, width)
    queries, kv = heads_into(projected, projected, projected, inv, gain_q, gain_k, cosine, sine)
    inv_c = lax.rsqrt(sums_c / D + EPSILON)[:, None]
    unit_c = ck_raw * inv_c
    cap_keys = (unit_c * gain_c).astype(LOW)
    cap_values = caption_mine[:, width:].astype(LOW)
    kv_far = far(kv)

    near, away, back_away, back_near = attention_calls(square, width, capt, t_size - 1)
    out_near, out_cross, stats = near(queries, kv, kv, cap_keys, cap_values, seg_col, seg_row)
    out_self, mixed, lse = away(queries, kv_far, kv_far, seg_col, seg_far, out_near, out_cross, stats, gate_row)
    mixed_both = two_cores(mixed)
    attended = scatter_square(dot(mixed, outw))

    clip_here = segment_here[:, None] == 0
    scale_attn = per_token(modulation[:, :D], clip_here)
    gate_attn = jnp.tanh(per_token(modulation[:, D : 2 * D], clip_here))
    scale_ffn = per_token(modulation[:, 2 * D : 3 * D], clip_here)
    gate_ffn = jnp.tanh(per_token(modulation[:, 3 * D :], clip_here))
    attn_unit = unit_rows(attended)
    middle = source + gate_attn * attn_unit * gains[1]
    unit_mid = unit_rows(middle)
    second_low = (unit_mid * gains[2] * (1.0 + scale_ffn)).astype(LOW)
    second_in = gather_square(second_low)
    hidden_units = FF // 4
    gate_values = dot(second_in, gate_up_mine)
    gate_part, up_part = gate_values[:, :hidden_units], gate_values[:, hidden_units:]
    activated = (jax.nn.silu(gate_part) * up_part).astype(LOW)
    activated_both = two_cores(activated)
    lowered = scatter_square(dot(activated, down_mine))
    low_unit = unit_rows(lowered)
    result = middle + gate_ffn * low_unit * gains[3]

    upstream = mirror(cotangent).astype(F32)
    d_gate_ffn = upstream * low_unit * gains[3] * (1.0 - gate_ffn * gate_ffn)
    d_lowered, grad_gain3 = norm_back(upstream * gate_ffn, lowered, gains[3])
    d_lowered_sq = gather_square(d_lowered.astype(LOW))
    d_activated = dot(d_lowered_sq, down_mine, ((1,), (1,)))
    sigmoid = jax.nn.sigmoid(gate_part)
    d_gate_part = d_activated * up_part * sigmoid * (1.0 + gate_part * (1.0 - sigmoid))
    d_up_part = d_activated * gate_part * sigmoid
    d_gate_values = jnp.concatenate([d_gate_part, d_up_part], 1).astype(LOW)
    d_second = scatter_square(dot(d_gate_values, gate_up_mine, ((1,), (1,))))

    down_sum = grad_columns(activated_both, two_cores_half(d_lowered_sq))
    up_terms = grad_product(second_in, d_gate_values, 4)
    up_terms = jnp.stack([row_blocks(up_terms[q]) for q in range(4)]) if lead else up_terms
    up_terms = up_terms.reshape((4 * outer, D // outer) + up_terms.shape[-1:])
    up_rows = lax.psum_scatter(up_terms, ("core", "x", "o"), scatter_dimension=0)
    up_rows = up_rows.reshape(4, gate_up.shape[0], -1)

    d_scale_ffn = d_second * unit_mid * gains[2]
    d_middle_norm, grad_gain2 = norm_back(d_second * (1.0 + scale_ffn), middle, gains[2])
    d_middle = upstream + d_middle_norm
    d_gate_attn = d_middle * attn_unit * gains[1] * (1.0 - gate_attn * gate_attn)
    d_attended, grad_gain1 = norm_back(d_middle * gate_attn, attended, gains[1])

    d_attended_sq = gather_square(d_attended.astype(LOW))
    d_mixed = dot(d_attended_sq, outw, ((1,), (1,))).astype(LOW)
    dq_part, dkv_far, dck, dcv, d_head, delta = back_away(
        queries, d_mixed, out_self, out_cross, lse, stats, gate_row, kv_far, kv_far, cap_keys,
        cap_values, seg_col, seg_far,
    )
    far_terms = [lax.ppermute(dkv_far[r - 1], t_axis, [(i, i ^ r) for i in range(t_size)]) for r in range(1, t_size)]
    d_query, dk_near, dv_near = back_near(queries, d_mixed, lse, delta, kv, kv, seg_col, seg_row, dq_part)
    dkv_other = far_terms[0] if t_size == 2 else sum(term.astype(F32) for term in far_terms)
    d_cap = axis_sum(jnp.concatenate([dck, dcv], 1), t_axis)
    out_sum = grad_columns(mixed_both, two_cores_half(d_attended_sq))
    inner_q, inner_k, head_sums, gain_qk = heads_out(
        d_query, dk_near, dkv_other, projected, projected, inv, gain_q, gain_k, cosine, sine
    )
    inner_c = d_cap[:, :width] * gain_c
    sums, sums_c = square_sum(jnp.sum(head_sums, 0).T, jnp.sum(inner_c * unit_c, -1))
    mean = (sums / D).T
    d_q_raw = inv[:, 0:1] * (inner_q - q_raw * inv[:, 0:1] * mean[:, 0:1])
    d_k_raw = inv[:, 1:2] * (inner_k - k_raw * inv[:, 1:2] * mean[:, 1:2])
    d_value = dv_near + dkv_other[1].astype(F32)
    d_projected = jnp.concatenate([d_q_raw, d_k_raw, d_value], 1).astype(LOW)
    rows_qkv = qkv_weight.shape[0]
    quarter = rows_qkv // 4
    qkv_part = dot(first_in, d_projected, ((0,), (0,))).astype(LOW)
    qkv_part = row_blocks(qkv_part).reshape(outer, 4, 2, 2, quarter, -1)
    qkv_core = swap(lax.dynamic_index_in_dim(qkv_part, 1 - core, 3, keepdims=False), "core")
    qkv_own = lax.dynamic_index_in_dim(qkv_part, core, 3, keepdims=False)
    qkv_part = (qkv_own.astype(F32) + qkv_core.astype(F32)).astype(LOW)
    qkv_x = swap(lax.dynamic_index_in_dim(qkv_part, 1 - me_x, 2, keepdims=False), "x")
    qkv_own = lax.dynamic_index_in_dim(qkv_part, me_x, 2, keepdims=False)
    qkv_part = (qkv_own.astype(F32) + qkv_x.astype(F32)).astype(LOW)
    d_first = scatter_square(dot(hold(d_projected, qkv_core), qkv_mine, ((1,), (1,))))
    after_heads = when(d_projected)
    half_outer = outer // 2
    f = FF // blk
    up_low = jnp.zeros((gate_up.shape[0], 4 * up_rows.shape[2]), LOW)
    for r in range(4):
        piece = lax.dynamic_index_in_dim(up_rows, (me_c ^ r) + after_heads, 0, keepdims=False)
        piece = to_place(piece, r) if r else piece
        for j in range(half_outer):
            up_low = lax.dynamic_update_slice(up_low, piece[:, j * f : (j + 1) * f], (0, (j * 4 + (me_c ^ r)) * f))
    up_half = pair_stack(hold(up_low, qkv_x), "x", 1)
    grad_gate_up = pair_stack(up_half, "core", 1).astype(F32)
    if lead:
        grad_gate_up = unblocks(grad_gate_up.reshape(-1, 2, outer, 4, f)).reshape(gate_up.shape)


    qkv_part = low(outer_reduce(qkv_part))
    qkv_summed = qkv_part
    qkv_part = [
        to_place(lax.dynamic_index_in_dim(qkv_part, me_c ^ r, 0, keepdims=False), r) for r in range(4)
    ]
    qkv_part = lay(qkv_part, 3)
    qkv_part = pair_stack(qkv_part[None], "x", 0)
    qkv_other = swap(qkv_part, "core")
    grad_qkv = jnp.stack([jnp.where(core == i, qkv_part, qkv_other) for i in range(2)], 1)
    grad_qkv = grad_qkv.reshape(rows_qkv, -1).astype(F32)


    d_c_raw = inv_c * (inner_c - unit_c * (sums_c / D)[:, None])
    d_cap_mine = jnp.concatenate([d_c_raw, d_cap[:, width:]], 1).astype(LOW)
    cap_blocks = gather_places(hold(mirror(d_cap_mine), qkv_x))
    d_cap_low = lay(cap_blocks, 2)
    grad_caption = finish(low(grad_columns(two_cores(chosen_rows), two_cores_half(d_cap_low))), 1)
    d_chosen = dot(d_cap_low, caption_weight, ((1,), (1,))).reshape(CLIPS, CAP, -1)
    grad_null = jnp.sum(jnp.where(dropped[:, None, None] == 1, d_chosen, 0.0), 0)
    grad_null = rounded(grad_null) + swap(low(grad_null), "core").astype(F32)
    grad_null = rounded(grad_null) + swap(low(grad_null), "x").astype(F32)

    unit_in = unit_rows(source)
    d_scale_attn = d_first * unit_in * gains[0]
    d_source_norm, grad_gain0 = norm_back(d_first * (1.0 + scale_attn), source, gains[0])
    input_grad = d_middle + d_source_norm
    if mirrored:
        input_grad = jnp.where(core == me_o, input_grad, mirror(input_grad.astype(LOW)).astype(F32))
        result = jnp.where(core == me_o, result, mirror(result.astype(LOW)).astype(F32))

    onehot = (segment_here[:, None] == jnp.arange(CLIPS)[None, :]).astype(F32)

    def per_clip(grad):
        return lax.dot_general(onehot, grad, (((0,), (0,)), ((), ())), precision=PRECISE)

    grad_gain6 = jnp.where(me_t == 0, jnp.sum(d_cap[:, :width] * unit_c, 0), 0.0)
    placed = lay([jnp.concatenate([gain_qk, grad_gain6[None], d_head])], 1)
    small = jnp.concatenate(
        [
            per_clip(d_scale_attn),
            per_clip(d_gate_attn),
            per_clip(d_scale_ffn),
            per_clip(d_gate_ffn),
            grad_gain0[None],
            grad_gain1[None],
            grad_gain2[None],
            grad_gain3[None],
            placed,
        ]
    )
    small = low(hold(sum_over(small, t_axis, "y", "p"), qkv_summed))
    small_x = pair_stack(small[None], "x", 0)
    small = pair_stack(small_x[None], g_axis, 0)
    rows_low = low(
        jnp.concatenate(
            [outer_reduce(v.reshape(outer, -1, D // 4)) for v in (hold(down_sum, qkv_core), hold(out_sum, qkv_core))]
        )
    )

    rows_done = finish(hold(rows_low, small_x), 1)
    grad_down, grad_out = rows_done[: down_weight.shape[0]], rows_done[down_weight.shape[0] :]
    count = 4 * CLIPS
    d_mod = jnp.concatenate([small[:, :, CLIPS * i : CLIPS * (i + 1)] for i in range(4)], -1).reshape(-1, 4 * D)
    grad_ada = dot(cond_all, d_mod, ((0,), (0,)))
    grad_ada_b = jnp.sum(d_mod.astype(F32), 0)
    sums = jnp.sum(small[:, :, count : count + 8].astype(F32), (0, 1))
    grad_gains = sums[:7]
    grad_head = jnp.sum(sums[7].reshape(HEADS, HEAD), -1) * (1.0 - head_tanh * head_tanh)
    return (
        result,
        input_grad,
        grad_ada,
        grad_ada_b,
        grad_qkv,
        grad_out,
        grad_caption,
        grad_gate_up,
        grad_down,
        grad_null,
        grad_gains,
        grad_head,
    )


def solution(mesh):
    devices = mesh.devices
    outer = devices.shape[1] // 4
    lead = (D // devices.shape[1]) % HEAD != 0
    if lead:
        grid = Mesh(devices.reshape(2, 2, 2, 2, outer), ("x", "core", "p", "y", "o"))
        blk = ("p", "y", "o")
    else:
        grid = Mesh(devices.reshape(2, 2, outer, 2, 2), ("x", "core", "o", "p", "y"))
        blk = ("o", "p", "y")
    dp = ("x", "core")
    every = dp + blk
    in_specs = (
        P(every, None),
        P(every),
        P(None, every),
        P(dp, None),
        P(dp, None, blk),
        P(dp),
        P(None, blk),
        P(blk, None),
        P(),
        P(blk, None),
        P(blk, None),
        P(blk, None),
        P(blk, None),
        P(blk, None),
        P(),
        P(),
        P(every, None),
    )
    out_specs = (
        P(every, None),
        P(every, None),
        P(blk, None),
        P(),
        P(blk, None),
        P(blk, None),
        P(blk, None),
        P(blk, None),
        P(blk, None),
        P(None, blk),
        P(),
        P(),
    )
    return jax.shard_map(
        functools.partial(on_device, outer, lead),
        mesh=grid,
        in_specs=in_specs,
        out_specs=out_specs,
        check_vma=False,
    )
```

```python
import functools

import jax
import jax.numpy as jnp
from jax import lax
from jax.experimental import pallas as pl
from jax.experimental.pallas import tpu as pltpu
from jax.sharding import Mesh, PartitionSpec as P

HEADS = 24
HEAD = 64
D = 1536
FF = 4096
CAP = 128
CLIPS = 2
PAIR = 2 * HEAD

PRECISE = lax.Precision.HIGHEST
EPSILON = 1e-06
NEGATIVE = -1e30
F32 = jnp.float32
LOW = jnp.bfloat16
SWAP = [(0, 1), (1, 0)]


def inv_root(values):
    return lax.rsqrt(jnp.mean(values * values, -1, keepdims=True) + EPSILON)


def unit_rows(values):
    return values * inv_root(values)


def norm_back(grad_in, values, gain):
    root = inv_root(values)
    normed = values * root
    inner = grad_in * gain
    back = root * (inner - normed * jnp.mean(inner * normed, -1, keepdims=True))
    return back, jnp.sum(grad_in * normed, 0)


def rounded(values):
    return lax.reduce_precision(values, 8, 7)


def low(values):
    return rounded(values).astype(LOW)


def dot(a, b, dims=((1,), (0,))):
    return lax.dot_general(a, b, (dims, ((), ())), preferred_element_type=F32)


def nt(a, b):
    return lax.dot_general(a, b, (((1,), (1,)), ((), ())), preferred_element_type=F32)


def tn(a, b):
    return lax.dot_general(a, b, (((0,), (0,)), ((), ())), preferred_element_type=F32)


def nn(a, b):
    return lax.dot_general(a, b, (((1,), (0,)), ((), ())), preferred_element_type=F32)


def cross_bias(seg_col, count):
    clip = lax.broadcasted_iota(jnp.int32, (1, count), 1) // CAP
    return jnp.where(seg_col == clip, 0.0, NEGATIVE)


def forward_near(q_ref, k_ref, v_ref, ck_ref, cv_ref, sq_ref, sk_ref, o_ref, oc_ref, st_ref):
    seg_col = sq_ref[...]
    bias = jnp.where(seg_col == sk_ref[...], 0.0, NEGATIVE)
    bias_cross = cross_bias(seg_col, ck_ref.shape[0])
    for h in range(2):
        at = slice(h * HEAD, (h + 1) * HEAD)
        q = q_ref[:, at]
        s = nt(q, k_ref[:, at]) + bias
        m = jnp.max(s, -1, keepdims=True)
        e = jnp.exp(s - m)
        st_ref[0, :, h : h + 1] = m
        st_ref[0, :, 2 + h : 3 + h] = jnp.sum(e, -1, keepdims=True)
        o_ref[:, at] = nn(e.astype(LOW), v_ref[:, at])
        s = nt(q, ck_ref[:, at]) + bias_cross
        m = jnp.max(s, -1, keepdims=True)
        e = jnp.exp(s - m)
        total = jnp.sum(e, -1, keepdims=True)
        st_ref[0, :, 4 + h : 5 + h] = m + jnp.log(total)
        oc_ref[:, at] = nn(e.astype(LOW), cv_ref[:, at]) / total


def forward_far(
    count, q_ref, k_ref, v_ref, sq_ref, sk_ref, o_ref, oc_ref, st_ref, gate_ref, os_ref, mix_ref, lse_ref, m_ref, l_ref
):
    step = pl.program_id(1)

    @pl.when(step == 0)
    def _():
        os_ref[...] = o_ref[...]
        m_ref[...] = st_ref[0, :, 0:2]
        l_ref[...] = st_ref[0, :, 2:4]

    bias = jnp.where(sq_ref[...] == sk_ref[0], 0.0, NEGATIVE)
    for h in range(2):
        at = slice(h * HEAD, (h + 1) * HEAD)
        s = nt(q_ref[:, at], k_ref[0, :, at]) + bias
        before = m_ref[:, h : h + 1]
        m = jnp.maximum(before, jnp.max(s, -1, keepdims=True))
        e = jnp.exp(s - m)
        factor = jnp.exp(before - m)
        m_ref[:, h : h + 1] = m
        l_ref[:, h : h + 1] = l_ref[:, h : h + 1] * factor + jnp.sum(e, -1, keepdims=True)
        os_ref[:, at] = os_ref[:, at] * factor + nn(e.astype(LOW), v_ref[0, :, at])

    @pl.when(step == count - 1)
    def _():
        for h in range(2):
            at = slice(h * HEAD, (h + 1) * HEAD)
            total = l_ref[:, h : h + 1]
            out = os_ref[:, at] / total
            os_ref[:, at] = out
            mix_ref[:, at] = (out + gate_ref[:, at] * oc_ref[:, at]).astype(LOW)
            lse_ref[0, :, h : h + 1] = m_ref[:, h : h + 1] + jnp.log(total)


def backward_far(
    q_ref, g_ref, os_ref, oc_ref, lse_ref, st_ref, gate_ref, k_ref, v_ref, ck_ref, cv_ref, sq_ref, sk_ref,
    dq_ref, dkv_ref, dck_ref, dcv_ref, dh_ref, delta_ref,
):
    step = pl.program_id(1)
    seg_col = sq_ref[...]
    scaling = HEAD**-0.5

    @pl.when(step == 0)
    def _():
        bias_cross = cross_bias(seg_col, ck_ref.shape[0])
        g = g_ref[...].astype(F32)
        dh_ref[...] = jnp.sum(g * oc_ref[...], 0, keepdims=True)
        for h in range(2):
            at = slice(h * HEAD, (h + 1) * HEAD)
            gh = g[:, at]
            delta_ref[0, :, h : h + 1] = jnp.sum(gh * os_ref[:, at], -1, keepdims=True)
            gc = (gate_ref[:, at] * gh).astype(LOW)
            delta = jnp.sum(gc.astype(F32) * oc_ref[:, at], -1, keepdims=True)
            q = q_ref[:, at]
            p = jnp.exp(nt(q, ck_ref[:, at]) + bias_cross - st_ref[0, :, 4 + h : 5 + h])
            ds = (p * (nt(gc, cv_ref[:, at]) - delta)).astype(LOW)
            dq_ref[:, at] = nn(ds, ck_ref[:, at]) * scaling
            dck_ref[:, at] = tn(ds, q).astype(dck_ref.dtype)
            dcv_ref[:, at] = tn(p.astype(LOW), gc).astype(dcv_ref.dtype)

    bias = jnp.where(seg_col == sk_ref[0], 0.0, NEGATIVE)
    for h in range(2):
        at = slice(h * HEAD, (h + 1) * HEAD)
        q = q_ref[:, at]
        g = g_ref[:, at]
        k = k_ref[0, :, at]
        p = jnp.exp(nt(q, k) + bias - lse_ref[0, :, h : h + 1])
        ds = (p * (nt(g, v_ref[0, :, at]) - delta_ref[0, :, h : h + 1])).astype(LOW)
        dq_ref[:, at] += nn(ds, k) * scaling
        dkv_ref[0, 0, :, at] = tn(ds, q).astype(LOW)
        dkv_ref[0, 1, :, at] = tn(p.astype(LOW), g).astype(LOW)


def backward_near(q_ref, g_ref, lse_ref, delta_ref, k_ref, v_ref, sq_ref, sk_ref, dp_ref, dq_ref, dk_ref, dv_ref):
    bias = jnp.where(sq_ref[...] == sk_ref[...], 0.0, NEGATIVE)
    scaling = HEAD**-0.5
    for h in range(2):
        at = slice(h * HEAD, (h + 1) * HEAD)
        q = q_ref[:, at]
        g = g_ref[:, at]
        k = k_ref[:, at]
        p = jnp.exp(nt(q, k) + bias - lse_ref[0, :, h : h + 1])
        ds = (p * (nt(g, v_ref[:, at]) - delta_ref[0, :, h : h + 1])).astype(LOW)
        dq_ref[:, at] = dp_ref[:, at] + nn(ds, k) * scaling
        dk_ref[:, at] = tn(ds, q)
        dv_ref[:, at] = tn(p.astype(LOW), g)


def swapped(x):
    lane = lax.broadcasted_iota(jnp.int32, x.shape, 1)
    return jnp.where(lane % 2 == 0, pltpu.roll(x, x.shape[1] - 1, 1), pltpu.roll(x, 1, 1))


def heads_in(q_ref, k_ref, v_ref, inv_ref, gq_ref, gk_ref, cos_ref, sin_ref, q_out, kv_out):
    cosine, sine = cos_ref[...], sin_ref[...]
    q = q_ref[...] * inv_ref[:, 0:1] * gq_ref[...]
    k = k_ref[...] * inv_ref[:, 1:2] * gk_ref[...]
    q = (q * cosine + swapped(q) * sine).astype(LOW)
    q_out[...] = (q.astype(F32) * HEAD**-0.5).astype(LOW)
    kv_out[0] = (k * cosine + swapped(k) * sine).astype(LOW)
    kv_out[1] = v_ref[...].astype(LOW)


def heads_back(
    dq_ref, dk_ref, far_ref, q_ref, k_ref, inv_ref, gq_ref, gk_ref, cos_ref, sin_ref, iq_out, ik_out, st_out, gg_out
):
    cosine, sine = cos_ref[...], sin_ref[...]
    dq = dq_ref[...]
    dk = dk_ref[...] + far_ref[0].astype(F32)
    uq = q_ref[...] * inv_ref[:, 0:1]
    uk = k_ref[...] * inv_ref[:, 1:2]
    tq = dq * cosine - swapped(dq) * sine
    tk = dk * cosine - swapped(dk) * sine
    gg_out[0:1] = jnp.sum(tq * uq, 0, keepdims=True)
    gg_out[1:2] = jnp.sum(tk * uk, 0, keepdims=True)
    iq = tq * gq_ref[...]
    ik = tk * gk_ref[...]
    iq_out[...] = iq
    ik_out[...] = ik
    st_out[0, :, 0:1] = jnp.sum(iq * uq, -1, keepdims=True)
    st_out[0, :, 1:2] = jnp.sum(ik * uk, -1, keepdims=True)


def head_calls(tokens, width):
    pairs = width // PAIR
    sds = jax.ShapeDtypeStruct

    def at(first):
        return pl.BlockSpec((tokens, PAIR), lambda i: (0, first + i))

    row = pl.BlockSpec((1, PAIR), lambda i: (0, i))
    fixed = pl.BlockSpec((tokens, PAIR), lambda i: (0, 0))
    inv = pl.BlockSpec((tokens, 2), lambda i: (0, 0))
    both = pl.BlockSpec((2, tokens, PAIR), lambda i: (0, 0, i))
    cost = pl.CostEstimate(flops=20 * tokens * width, bytes_accessed=20 * tokens * width, transcendentals=0)
    into = pl.pallas_call(
        heads_in,
        grid=(pairs,),
        in_specs=[at(0), at(pairs), at(2 * pairs), inv, row, row, fixed, fixed],
        out_specs=[at(0), both],
        out_shape=[sds((tokens, width), LOW), sds((2, tokens, width), LOW)],
        cost_estimate=cost,
        name="heads_in",
    )
    back = pl.pallas_call(
        heads_back,
        grid=(pairs,),
        in_specs=[at(0), at(0), pl.BlockSpec((1, tokens, PAIR), lambda i: (0, 0, i)), at(0), at(pairs), inv, row, row, fixed, fixed],
        out_specs=[at(0), at(0), pl.BlockSpec((1, tokens, 2), lambda i: (i, 0, 0)), pl.BlockSpec((2, PAIR), lambda i: (0, i))],
        out_shape=[sds((tokens, width), F32), sds((tokens, width), F32), sds((pairs, tokens, 2), F32), sds((2, width), F32)],
        cost_estimate=cost,
        name="heads_back",
    )
    return into, back


def place_columns(place, groups, outer, rest, lead):
    whole = 4 * outer * rest
    return [
        g * whole + ((place * outer + o) if lead else (o * 4 + place)) * rest for g in range(groups) for o in range(outer)
    ]


def cut_kernel(columns, rest, me_ref, x_ref, *outs):
    for me in range(4):

        @pl.when(me_ref[0] == me)
        def _():
            for r, out in enumerate(outs):
                for j, start in enumerate(columns[me ^ r]):
                    out[:, j * rest : (j + 1) * rest] = x_ref[:, start : start + rest]


def lay_kernel(columns, rest, blank, me_ref, *refs):
    ins, out = refs[:-1], refs[-1]
    if blank:
        out[...] = jnp.zeros_like(out)
    for me in range(4):

        @pl.when(me_ref[0] == me)
        def _():
            for r, value in enumerate(ins):
                for j, start in enumerate(columns[me ^ r]):
                    out[:, start : start + rest] = value[:, j * rest : (j + 1) * rest]


def caption_kernel(columns, rest, rows_ref, weight_ref, out_ref):
    product = nn(rows_ref[...], weight_ref[...])
    for place in range(4):
        for j, start in enumerate(columns[place]):
            out_ref[place, :, j * rest : (j + 1) * rest] = product[:, start : start + rest].astype(out_ref.dtype)


def assemble_kernel(plan, width, at_ref, *refs):
    ins, out, sems = refs[:-2], refs[-2], refs[-1]
    copies = []
    for i, (source, first, rows) in enumerate(plan):
        row = pl.multiple_of(at_ref[2 * i], 16)
        col = pl.multiple_of(at_ref[2 * i + 1], 128)
        copies.append(
            pltpu.make_async_copy(
                ins[source].at[pl.ds(first, rows)], out.at[pl.ds(row, rows), pl.ds(col, width)], sems.at[i]
            )
        )
    for copy in copies:
        copy.start()
    for copy in copies:
        copy.wait()


def product_kernel(left_ref, right_ref, out_ref):
    out_ref[0] = tn(left_ref[...], right_ref[...]).astype(out_ref.dtype)


def grad_product(left, right, parts):
    rows, cols = left.shape[1], right.shape[1] // parts
    tile = 512 if rows % 512 == 0 else rows
    return pl.pallas_call(
        product_kernel,
        grid=(parts, rows // tile),
        in_specs=[
            pl.BlockSpec((left.shape[0], tile), lambda q, i: (0, i)),
            pl.BlockSpec((left.shape[0], cols), lambda q, i: (0, q)),
        ],
        out_specs=pl.BlockSpec((1, tile, cols), lambda q, i: (q, i, 0)),
        out_shape=jax.ShapeDtypeStruct((parts, rows, cols), LOW),
        cost_estimate=pl.CostEstimate(
            flops=2 * left.shape[0] * rows * right.shape[1],
            bytes_accessed=2 * (rows * right.shape[1] + left.size + right.size),
            transcendentals=0,
        ),
        compiler_params=pltpu.CompilerParams(fuse_transposed_lhs_in_matmul=True),
        name="grad_product",
    )(left, right)


def assemble(inputs, plan, places, shape):
    width = inputs[0].shape[1]
    at = jnp.stack([jnp.asarray(v, jnp.int32) for pair in places for v in pair])
    size = 2 * shape[0] * shape[1] * 2
    return pl.pallas_call(
        functools.partial(assemble_kernel, plan, width),
        grid_spec=pltpu.PrefetchScalarGridSpec(
            num_scalar_prefetch=1,
            grid=(1,),
            in_specs=[pl.BlockSpec(memory_space=pl.ANY)] * len(inputs),
            out_specs=pl.BlockSpec(memory_space=pltpu.VMEM),
            scratch_shapes=[pltpu.SemaphoreType.DMA((len(plan),))],
        ),
        out_shape=jax.ShapeDtypeStruct(shape, inputs[0].dtype),
        compiler_params=pltpu.CompilerParams(vmem_limit_bytes=32 * 1024 * 1024),
        cost_estimate=pl.CostEstimate(flops=0, bytes_accessed=size, transcendentals=0),
        name="assemble",
    )(at, *inputs)


def attention_calls(tokens, width, capt, far):
    pairs = width // PAIR
    sds = jax.ShapeDtypeStruct

    def cols(rows):
        return pl.BlockSpec((rows, PAIR), lambda i, *r: (0, i))

    def stat(n):
        return pl.BlockSpec((1, tokens, n), lambda i, *r: (i, 0, 0))

    seg_col = pl.BlockSpec((tokens, 1), lambda i, *r: (0, 0))
    seg_row = pl.BlockSpec((1, tokens), lambda i, *r: (0, 0))
    far_k = pl.BlockSpec((1, None, tokens, PAIR), lambda i, r: (r, 0, 0, i))
    far_v = pl.BlockSpec((1, None, tokens, PAIR), lambda i, r: (r, 1, 0, i))
    far_both = pl.BlockSpec((1, 2, tokens, PAIR), lambda i, r: (r, 0, 0, i))
    near_k = pl.BlockSpec((None, tokens, PAIR), lambda i, *r: (0, 0, i))
    near_v = pl.BlockSpec((None, tokens, PAIR), lambda i, *r: (1, 0, i))
    far_row = pl.BlockSpec((1, 1, tokens), lambda i, r: (r, 0, 0))
    gate = cols(1)
    tok, cap = cols(tokens), cols(capt)

    def cost(keys, products):
        return pl.CostEstimate(
            flops=2 * tokens * keys * width * products,
            bytes_accessed=8 * tokens * width * 4,
            transcendentals=tokens * keys * (width // HEAD),
        )

    params = pltpu.CompilerParams(vmem_limit_bytes=48 * 1024 * 1024)
    near = pl.pallas_call(
        forward_near,
        grid=(pairs,),
        in_specs=[tok, near_k, near_v, cap, cap, seg_col, seg_row],
        out_specs=[tok, tok, stat(8)],
        out_shape=[sds((tokens, width), F32), sds((tokens, width), F32), sds((pairs, tokens, 8), F32)],
        compiler_params=params,
        cost_estimate=cost(tokens + capt, 2),
        name="attn_near",
    )
    away = pl.pallas_call(
        functools.partial(forward_far, far),
        grid=(pairs, far),
        in_specs=[tok, far_k, far_v, seg_col, far_row, tok, tok, stat(8), gate],
        out_specs=[tok, tok, stat(2)],
        out_shape=[sds((tokens, width), F32), sds((tokens, width), LOW), sds((pairs, tokens, 2), F32)],
        scratch_shapes=[pltpu.VMEM((tokens, 2), F32), pltpu.VMEM((tokens, 2), F32)],
        compiler_params=params,
        cost_estimate=cost(tokens * far, 2),
        name="attn_far",
    )
    back_away = pl.pallas_call(
        backward_far,
        grid=(pairs, far),
        in_specs=[tok, tok, tok, tok, stat(2), stat(8), gate, far_k, far_v, cap, cap, seg_col, far_row],
        out_specs=[tok, far_both, cap, cap, gate, stat(2)],
        out_shape=[
            sds((tokens, width), F32),
            sds((far, 2, tokens, width), LOW),
            sds((capt, width), F32),
            sds((capt, width), F32),
            sds((1, width), F32),
            sds((pairs, tokens, 2), F32),
        ],
        compiler_params=params,
        cost_estimate=cost(tokens * far + capt, 5),
        name="attn_back_far",
    )
    back_near = pl.pallas_call(
        backward_near,
        grid=(pairs,),
        in_specs=[tok, tok, stat(2), stat(2), near_k, near_v, seg_col, seg_row, tok],
        out_specs=[tok, tok, tok],
        out_shape=[sds((tokens, width), F32)] * 3,
        compiler_params=params,
        cost_estimate=cost(tokens, 5),
        name="attn_back_near",
    )
    return near, away, back_away, back_near


def swap(value, axis):
    return lax.ppermute(value, axis, SWAP)


def pair_stack(value, axis, dim):
    other = swap(value, axis)
    first = lax.axis_index(axis) == 0
    return jnp.concatenate([jnp.where(first, value, other), jnp.where(first, other, value)], dim)


def hold(value, *after):
    return lax.optimization_barrier((value, after))[0]


def on_device(
    outer,
    lead,
    hidden,
    segments,
    positions,
    condition,
    captions,
    dropped,
    null_caption,
    ada_weight,
    ada_bias,
    qkv_weight,
    out_weight,
    caption_weight,
    gate_up,
    down_weight,
    gains,
    head_gate,
    cotangent,
):
    me_c = lax.axis_index("p") * 2 + lax.axis_index("y")
    me_o = lax.axis_index("o")
    core = lax.axis_index("core")
    me_x = lax.axis_index("x")
    me_b = lax.axis_index(("p", "y", "o") if lead else ("o", "p", "y"))
    me_arg = me_c.reshape(1).astype(jnp.int32)
    tokens = hidden.shape[0]
    square = 4 * tokens
    width = D // 4
    capt = CLIPS * CAP
    blk = 4 * outer
    rest = D // blk
    mirrored = outer == 2
    t_axis, g_axis = ("core", "o") if mirrored else ("o", "core")
    t_size = 2 if mirrored else outer
    me_t, me_g = lax.axis_index(t_axis), lax.axis_index(g_axis)
    across = [[(i, i ^ r) for i in range(4)] for r in range(4)]
    beyond = [[(i, i ^ r) for i in range(outer)] for r in range(outer)]

    def unblocks(value):
        if lead:
            value = value.swapaxes(-3, -2)
        return value.reshape(value.shape[:-3] + (-1,))

    def row_blocks(value):
        size = value.shape[0] // blk
        if lead:
            return value.reshape((4, outer, size) + value.shape[1:]).swapaxes(0, 1)
        return value.reshape((outer, 4, size) + value.shape[1:])

    def block_index(o, c):
        return c * outer + o if lead else o * 4 + c

    def cut(value, groups, count):
        size = value.shape[1] // (groups * blk)
        columns = [place_columns(c, groups, outer, size, lead) for c in range(4)]
        out = jax.ShapeDtypeStruct((value.shape[0], groups * outer * size), value.dtype)
        return pl.pallas_call(
            functools.partial(cut_kernel, columns, size),
            in_specs=[pl.BlockSpec(memory_space=pltpu.SMEM), pl.BlockSpec(memory_space=pltpu.VMEM)],
            out_specs=[pl.BlockSpec(memory_space=pltpu.VMEM)] * count,
            out_shape=[out] * count,
            name="cut",
        )(me_arg, value)

    def lay(pieces, groups):
        size = pieces[0].shape[1] // (groups * outer)
        columns = [place_columns(c, groups, outer, size, lead) for c in range(4)]
        shape = (pieces[0].shape[0], 4 * pieces[0].shape[1])
        return pl.pallas_call(
            functools.partial(lay_kernel, columns, size, len(pieces) < 4),
            in_specs=[pl.BlockSpec(memory_space=pltpu.SMEM)] + [pl.BlockSpec(memory_space=pltpu.VMEM)] * len(pieces),
            out_specs=pl.BlockSpec(memory_space=pltpu.VMEM),
            out_shape=jax.ShapeDtypeStruct(shape, pieces[0].dtype),
            name="lay",
        )(me_arg, *pieces)

    def outer_reduce(value):
        if outer == 2:
            sent = lax.dynamic_index_in_dim(value, 1 - me_o, 0, keepdims=False).astype(LOW)
            kept = lax.dynamic_index_in_dim(value, me_o, 0, keepdims=False)
            return kept.astype(F32) + swap(sent, "o").astype(F32)
        return lax.psum_scatter(value.astype(LOW), "o", scatter_dimension=0).astype(F32)

    def axis_sum(value, axis):
        if axis != "o" or outer == 2:
            return rounded(value) + swap(low(value), axis).astype(F32)
        return lax.psum(low(value), axis).astype(F32)

    def mirror(value):
        if not mirrored:
            return value
        other = lax.ppermute(value, ("core", "o"), [(1, 2), (2, 1)])
        return jnp.where(core == me_o, value, other)

    def far(value):
        return jnp.stack([lax.ppermute(value, t_axis, [(i, i ^ r) for i in range(t_size)]) for r in range(1, t_size)])

    def to_place(value, r):
        return lax.ppermute(value, ("p", "y"), across[r])

    def gather_places(rows):
        return [rows] + [to_place(rows, r) for r in (1, 2, 3)]

    def gather_square(rows):
        return jnp.concatenate(gather_places(rows))

    def scatter_places(parts):
        total = parts[0]
        for r in (1, 2, 3):
            total = total + to_place(parts[r].astype(LOW), r).astype(F32)
        return total

    def scatter_square(full):
        return scatter_places([full[r * tokens : (r + 1) * tokens] for r in range(4)])

    def square_sum(value, shared=None):
        count = 4 * value.shape[0]
        whole = value.reshape(count, tokens)
        if shared is not None:
            whole = jnp.concatenate([whole, shared.reshape(-1, tokens)])
        for axis, order in (("y", (1, 0, 3, 2)), ("p", (2, 3, 0, 1))):
            other = swap(whole, axis)
            order = [4 * i + j for i in range(value.shape[0]) for j in order]
            whole = whole + jnp.concatenate([other[i : i + 1] for i in order] + [other[count:]])
        sums = whole[:count].reshape(value.shape)
        return sums if shared is None else (sums, whole[count:].reshape(-1))

    def sum_over(value, *axes):
        for axis in axes:
            value = axis_sum(value, axis)
        return value

    def hand_on(own, split):
        pieces = [(own, 0, 0, 0)]
        if split:
            pieces += [(swap(own, "x"), 0, 1, 0)]
        for r in range(1, outer):
            far_piece = lax.ppermute(own, "o", beyond[r])
            pieces += [(far_piece, 0, 0, r)]
            if split:
                pieces += [(swap(far_piece, "x"), 0, 1, r)]
        if split:
            other = swap(jnp.concatenate([piece[0] for piece in pieces]), "core")
            size = own.shape[0]
            pieces += [(other[i * size : (i + 1) * size], 1, x, o) for i, (_, _, x, o) in enumerate(pieces)]
        return pieces

    def fetch_qkv(weight, after):
        rows = weight.shape[0]
        split = (rows // 4) % 16 == 0
        quarter = rows // 4 if split else rows
        if split:
            weight = lax.dynamic_slice_in_dim(weight, (me_x * 2 + core) * quarter, quarter, 0)
        cuts = cut(weight, 3, 4)
        arrived = [to_place(cuts[r], r) for r in (1, 2, 3)]
        pieces = hand_on(hold(jnp.concatenate([cuts[0]] + arrived), after), split)
        plan, places = [], []
        for i, (_, k, x, o) in enumerate(pieces):
            for r in range(4):
                plan.append((i, r * quarter, quarter))
                at = block_index(me_o ^ o, me_c ^ r) * rows
                places.append((at + ((me_x ^ x) * 2 + (core ^ k)) * quarter if split else at, 0))
        whole = assemble([piece[0] for piece in pieces], plan, places, (D, 3 * D // 4))
        return whole, pieces, arrived

    def start_gate_up(weight):
        rows = weight.shape[0]
        f = FF // blk

        def piece_of(r):
            cols = []
            for j in range(outer // 2):
                o = me_x * (outer // 2) + j
                at = core * FF + block_index(o, me_c ^ r) * f
                cols.append(lax.dynamic_slice(weight, (0, at), (rows, f)))
            return jnp.concatenate(cols, 1) if len(cols) > 1 else cols[0]

        arrived = [to_place(piece_of(r), r) for r in (1, 2, 3)]
        own = jnp.concatenate([piece_of(0)] + arrived)
        return own, arrived

    def fetch_gate_up(own):
        rows, n = own.shape[0] // 4, own.shape[1]
        whole = lax.all_gather(own, ("core", "x", "o"), axis=0, tiled=True)
        plan, places = [], []
        for q in range(4):
            for o in range(outer):
                for r in range(4):
                    plan.append((0, ((q * outer + o) * 4 + r) * rows, rows))
                    places.append((block_index(o, me_c ^ r) * rows, q * n))
        return assemble([whole], plan, places, (D, 2 * FF // 4))

    def fetch_down(weight, after):
        rows, quarter = weight.shape[0], D // 4
        mine = lax.dynamic_slice(weight, (0, (core * 2 + me_x) * quarter), (rows, quarter))
        whole = lax.all_gather(hold(mine, after), ("core", "x", "o"), axis=0, tiled=True)
        plan = [(0, i * rows, rows) for i in range(4 * outer)]
        places = [(o * rows, q * quarter) for q in range(4) for o in range(outer)]
        return assemble([whole], plan, places, (outer * rows, D))

    def fetch_rows(weight):
        rows, quarter = weight.shape[0], D // 4
        mine = lax.dynamic_slice(weight, (0, (core * 2 + me_x) * quarter), (rows, quarter))
        pieces = hand_on(mine, True)
        plan = [(i, 0, rows) for i in range(len(pieces))]
        places = [((me_o ^ o) * rows, ((core ^ k) * 2 + (me_x ^ x)) * quarter) for _, k, x, o in pieces]
        return assemble([piece[0] for piece in pieces], plan, places, (outer * rows, D)), pieces

    def finish(part, dim):
        return pair_stack(pair_stack(part, "x", dim), "core", dim).astype(F32)

    def two_cores(value):
        return jnp.concatenate([value, swap(value, "core")])

    def two_cores_half(value):
        half = value.shape[1] // 2
        first = core == 0
        a, b = value[:, :half], value[:, half:]
        return jnp.concatenate([jnp.where(first, a, b), swap(jnp.where(first, b, a), "core")])

    def grad_columns(left_both, grad_both):
        half = grad_both.shape[1] // 2
        theirs = lax.dynamic_slice_in_dim(grad_both, (1 - me_x) * half, half, 1)
        mine = lax.dynamic_slice_in_dim(grad_both, me_x * half, half, 1)
        sent = swap(dot(left_both, theirs, ((0,), (0,))).astype(LOW), "x")
        return dot(left_both, mine, ((0,), (0,))) + sent.astype(F32)

    numbers = jnp.concatenate([segments[None], positions]).T.astype(LOW)
    numbers = jnp.pad(numbers, ((0, 0), (0, 128 - numbers.shape[1])))
    mine = mirror(jnp.concatenate([hidden, numbers], 1))
    source = mine[:, :D].astype(F32)
    segment_here = mine[:, D].astype(jnp.int32)
    chosen = jnp.where(dropped[:, None, None] == 1, null_caption[None], captions)
    chosen_rows = chosen.reshape(capt, chosen.shape[2])
    caption_parts = pl.pallas_call(
        functools.partial(caption_kernel, [place_columns(c, 2, outer, rest, lead) for c in range(4)], rest),
        out_shape=jax.ShapeDtypeStruct((4, capt, 2 * width), LOW),
        in_specs=[pl.BlockSpec(memory_space=pltpu.VMEM)] * 2,
        out_specs=pl.BlockSpec(memory_space=pltpu.VMEM),
        compiler_params=pltpu.CompilerParams(vmem_limit_bytes=40 * 1024 * 1024),
        cost_estimate=pl.CostEstimate(
            flops=2 * capt * chosen_rows.shape[1] * 2 * D, bytes_accessed=8 * 1024 * 1024, transcendentals=0
        ),
        name="caption_product",
    )(chosen_rows, caption_weight)
    caption_parts = [lax.dynamic_index_in_dim(caption_parts, me_c ^ r, 0, keepdims=False) for r in range(4)]
    caption_half = scatter_places([caption_parts[0].astype(F32)] + caption_parts[1:])

    cond_rows = ada_weight.shape[0]
    cond_low = lax.dynamic_slice_in_dim(jax.nn.silu(condition), me_b * cond_rows, cond_rows, 1).astype(LOW)
    cond_both = pair_stack(cond_low, "core", 0)
    cond_all = pair_stack(cond_both.reshape(2, 1, CLIPS, cond_rows), "x", 1).reshape(-1, cond_rows)
    modulation = sum_over(dot(cond_both, ada_weight), "o", "y", "p")
    modulation = lax.dynamic_slice_in_dim(modulation, me_g * CLIPS, CLIPS, 0) + ada_bias
    qkv_mine, qkv_pieces, qkv_arrived = fetch_qkv(qkv_weight, caption_half)
    tokens_blocks = gather_places(hold(mine, qkv_arrived, modulation))
    tokens_square = jnp.concatenate(tokens_blocks)
    hidden_square = tokens_square[:, :D].astype(F32)
    seg_square = tokens_square[:, D].astype(jnp.int32)
    pos_square = tokens_square[:, D + 1 : D + 4].astype(F32)
    seg_col, seg_row = seg_square[:, None], seg_square[None]
    seg_far = far(seg_row)

    qkv_here = qkv_pieces[2][0] if outer == 2 else qkv_pieces[-1][0]


    up_own, up_arrived = start_gate_up(hold(gate_up, tokens_blocks[3]))
    up_own = hold(up_own, qkv_here)


    head_tanh = jnp.tanh(head_gate)
    (place_gains,) = cut(jnp.concatenate([gains[4:7], jnp.repeat(head_tanh, HEAD)[None]]), 1, 1)
    gain_q, gain_k, gain_c, gate_row = (place_gains[i : i + 1] for i in range(4))

    pair_index = jnp.arange(PAIR) % HEAD // 2
    frequency = 10000.0 ** (-3.0 * (pair_index // 3).astype(F32) / (HEAD // 2))
    select = ((pair_index % 3)[None, :] == jnp.arange(3)[:, None]).astype(F32)
    angles = jnp.dot(pos_square, select, precision=PRECISE) * frequency[None, :]
    cosine = jnp.cos(angles)
    sine = jnp.sin(angles) * jnp.where(jnp.arange(PAIR) % 2 == 0, -1.0, 1.0)[None]

    def per_token(rows, sel):
        return jnp.where(sel, rows[0:1], rows[1:2])

    caption_mine = axis_sum(mirror(hold(caption_half, qkv_here).astype(LOW)).astype(F32), t_axis)
    scale_square = per_token(hold(modulation[:, :D], up_arrived, caption_mine, cosine), seg_col == 0)
    first_in = (unit_rows(hidden_square) * gains[0] * (1.0 + scale_square)).astype(LOW)
    projected = dot(first_in, qkv_mine)
    q_raw, k_raw = projected[:, :width], projected[:, width : 2 * width]
    ck_raw = caption_mine[:, :width]
    sums, sums_c = square_sum(
        jnp.stack([jnp.sum(q_raw * q_raw, -1), jnp.sum(k_raw * k_raw, -1)]), jnp.sum(ck_raw * ck_raw, -1)
    )
    outw, out_pieces = fetch_rows(hold(out_weight, qkv_here))
    gate_up_mine = fetch_gate_up(up_own)
    down_mine = fetch_down(down_weight, projected)
    inv = hold(lax.rsqrt(sums / D + EPSILON).T, seg_far, out_pieces[2][0])
    heads_into, heads_out = head_calls(square, width)
    queries, kv = heads_into(projected, projected, projected, inv, gain_q, gain_k, cosine, sine)
    inv_c = lax.rsqrt(sums_c / D + EPSILON)[:, None]
    unit_c = ck_raw * inv_c
    cap_keys = (unit_c * gain_c).astype(LOW)
    cap_values = caption_mine[:, width:].astype(LOW)
    kv_far = far(kv)

    near, away, back_away, back_near = attention_calls(square, width, capt, t_size - 1)
    out_near, out_cross, stats = near(queries, kv, kv, cap_keys, cap_values, seg_col, seg_row)
    out_self, mixed, lse = away(queries, kv_far, kv_far, seg_col, seg_far, out_near, out_cross, stats, gate_row)
    mixed_both = two_cores(mixed)
    attended = scatter_square(dot(mixed, outw))

    clip_here = segment_here[:, None] == 0
    scale_attn = per_token(modulation[:, :D], clip_here)
    gate_attn = jnp.tanh(per_token(modulation[:, D : 2 * D], clip_here))
    scale_ffn = per_token(modulation[:, 2 * D : 3 * D], clip_here)
    gate_ffn = jnp.tanh(per_token(modulation[:, 3 * D :], clip_here))
    attn_unit = unit_rows(attended)
    middle = source + gate_attn * attn_unit * gains[1]
    unit_mid = unit_rows(middle)
    second_low = (unit_mid * gains[2] * (1.0 + scale_ffn)).astype(LOW)
    second_in = gather_square(second_low)
    hidden_units = FF // 4
    gate_values = dot(second_in, gate_up_mine)
    gate_part, up_part = gate_values[:, :hidden_units], gate_values[:, hidden_units:]
    activated = (jax.nn.silu(gate_part) * up_part).astype(LOW)
    activated_both = two_cores(activated)
    lowered = scatter_square(dot(activated, down_mine))
    low_unit = unit_rows(lowered)
    result = middle + gate_ffn * low_unit * gains[3]

    upstream = mirror(cotangent).astype(F32)
    d_gate_ffn = upstream * low_unit * gains[3] * (1.0 - gate_ffn * gate_ffn)
    d_lowered, grad_gain3 = norm_back(upstream * gate_ffn, lowered, gains[3])
    d_lowered_sq = gather_square(d_lowered.astype(LOW))
    d_activated = dot(d_lowered_sq, down_mine, ((1,), (1,)))
    sigmoid = jax.nn.sigmoid(gate_part)
    d_gate_part = d_activated * up_part * sigmoid * (1.0 + gate_part * (1.0 - sigmoid))
    d_up_part = d_activated * gate_part * sigmoid
    d_gate_values = jnp.concatenate([d_gate_part, d_up_part], 1).astype(LOW)
    d_second = scatter_square(dot(d_gate_values, gate_up_mine, ((1,), (1,))))

    down_sum = grad_columns(activated_both, two_cores_half(d_lowered_sq))
    up_terms = grad_product(second_in, d_gate_values, 4)
    up_terms = jnp.stack([row_blocks(up_terms[q]) for q in range(4)]) if lead else up_terms
    up_terms = up_terms.reshape((4 * outer, D // outer) + up_terms.shape[-1:])
    up_rows = lax.psum_scatter(up_terms, ("core", "x", "o"), scatter_dimension=0)
    up_rows = up_rows.reshape(4, gate_up.shape[0], -1)

    d_scale_ffn = d_second * unit_mid * gains[2]
    d_middle_norm, grad_gain2 = norm_back(d_second * (1.0 + scale_ffn), middle, gains[2])
    d_middle = upstream + d_middle_norm
    d_gate_attn = d_middle * attn_unit * gains[1] * (1.0 - gate_attn * gate_attn)
    d_attended, grad_gain1 = norm_back(d_middle * gate_attn, attended, gains[1])

    d_attended_sq = gather_square(d_attended.astype(LOW))
    d_mixed = dot(d_attended_sq, outw, ((1,), (1,))).astype(LOW)
    dq_part, dkv_far, dck, dcv, d_head, delta = back_away(
        queries, d_mixed, out_self, out_cross, lse, stats, gate_row, kv_far, kv_far, cap_keys,
        cap_values, seg_col, seg_far,
    )
    far_terms = [lax.ppermute(dkv_far[r - 1], t_axis, [(i, i ^ r) for i in range(t_size)]) for r in range(1, t_size)]
    d_query, dk_near, dv_near = back_near(queries, d_mixed, lse, delta, kv, kv, seg_col, seg_row, dq_part)
    dkv_other = far_terms[0] if t_size == 2 else sum(term.astype(F32) for term in far_terms)
    d_cap = axis_sum(jnp.concatenate([dck, dcv], 1), t_axis)
    out_sum = grad_columns(mixed_both, two_cores_half(d_attended_sq))
    inner_q, inner_k, head_sums, gain_qk = heads_out(
        d_query, dk_near, dkv_other, projected, projected, inv, gain_q, gain_k, cosine, sine
    )
    inner_c = d_cap[:, :width] * gain_c
    sums, sums_c = square_sum(jnp.sum(head_sums, 0).T, jnp.sum(inner_c * unit_c, -1))
    mean = (sums / D).T
    d_q_raw = inv[:, 0:1] * (inner_q - q_raw * inv[:, 0:1] * mean[:, 0:1])
    d_k_raw = inv[:, 1:2] * (inner_k - k_raw * inv[:, 1:2] * mean[:, 1:2])
    d_value = dv_near + dkv_other[1].astype(F32)
    d_projected = jnp.concatenate([d_q_raw, d_k_raw, d_value], 1).astype(LOW)
    rows_qkv = qkv_weight.shape[0]
    quarter = rows_qkv // 4
    qkv_part = dot(first_in, d_projected, ((0,), (0,))).astype(LOW)
    qkv_part = row_blocks(qkv_part).reshape(outer, 4, 2, 2, quarter, -1)
    qkv_core = swap(lax.dynamic_index_in_dim(qkv_part, 1 - core, 3, keepdims=False), "core")
    qkv_own = lax.dynamic_index_in_dim(qkv_part, core, 3, keepdims=False)
    qkv_part = (qkv_own.astype(F32) + qkv_core.astype(F32)).astype(LOW)
    qkv_x = swap(lax.dynamic_index_in_dim(qkv_part, 1 - me_x, 2, keepdims=False), "x")
    qkv_own = lax.dynamic_index_in_dim(qkv_part, me_x, 2, keepdims=False)
    qkv_part = (qkv_own.astype(F32) + qkv_x.astype(F32)).astype(LOW)
    d_first = scatter_square(dot(hold(d_projected, qkv_core), qkv_mine, ((1,), (1,))))
    up_rows = hold(up_rows, d_projected)
    half_outer = outer // 2
    f = FF // blk
    up_low = jnp.zeros((gate_up.shape[0], 4 * up_rows.shape[2]), LOW)
    for r in range(4):
        piece = lax.dynamic_index_in_dim(up_rows, me_c ^ r, 0, keepdims=False)
        piece = to_place(piece, r) if r else piece
        for j in range(half_outer):
            up_low = lax.dynamic_update_slice(up_low, piece[:, j * f : (j + 1) * f], (0, (j * 4 + (me_c ^ r)) * f))
    up_half = pair_stack(hold(up_low, qkv_x), "x", 1)
    grad_gate_up = pair_stack(up_half, "core", 1).astype(F32)
    if lead:
        grad_gate_up = unblocks(grad_gate_up.reshape(-1, 2, outer, 4, f)).reshape(gate_up.shape)


    qkv_part = low(outer_reduce(qkv_part))
    qkv_summed = qkv_part
    qkv_part = [
        to_place(lax.dynamic_index_in_dim(qkv_part, me_c ^ r, 0, keepdims=False), r) for r in range(4)
    ]
    qkv_part = lay(qkv_part, 3)
    qkv_part = pair_stack(qkv_part[None], "x", 0)
    qkv_other = swap(qkv_part, "core")
    grad_qkv = jnp.stack([jnp.where(core == i, qkv_part, qkv_other) for i in range(2)], 1)
    grad_qkv = grad_qkv.reshape(rows_qkv, -1).astype(F32)


    d_c_raw = inv_c * (inner_c - unit_c * (sums_c / D)[:, None])
    d_cap_mine = jnp.concatenate([d_c_raw, d_cap[:, width:]], 1).astype(LOW)
    cap_blocks = gather_places(hold(mirror(d_cap_mine), qkv_x))
    d_cap_low = lay(cap_blocks, 2)
    grad_caption = finish(low(grad_columns(two_cores(chosen_rows), two_cores_half(d_cap_low))), 1)
    d_chosen = dot(d_cap_low, caption_weight, ((1,), (1,))).reshape(CLIPS, CAP, -1)
    grad_null = jnp.sum(jnp.where(dropped[:, None, None] == 1, d_chosen, 0.0), 0)
    grad_null = rounded(grad_null) + swap(low(grad_null), "core").astype(F32)
    grad_null = rounded(grad_null) + swap(low(grad_null), "x").astype(F32)

    unit_in = unit_rows(source)
    d_scale_attn = d_first * unit_in * gains[0]
    d_source_norm, grad_gain0 = norm_back(d_first * (1.0 + scale_attn), source, gains[0])
    input_grad = d_middle + d_source_norm
    if mirrored:
        input_grad = jnp.where(core == me_o, input_grad, mirror(input_grad.astype(LOW)).astype(F32))
        result = jnp.where(core == me_o, result, mirror(result.astype(LOW)).astype(F32))

    onehot = (segment_here[:, None] == jnp.arange(CLIPS)[None, :]).astype(F32)

    def per_clip(grad):
        return lax.dot_general(onehot, grad, (((0,), (0,)), ((), ())), precision=PRECISE)

    grad_gain6 = jnp.where(me_t == 0, jnp.sum(d_cap[:, :width] * unit_c, 0), 0.0)
    placed = lay([jnp.concatenate([gain_qk, grad_gain6[None], d_head])], 1)
    small = jnp.concatenate(
        [
            per_clip(d_scale_attn),
            per_clip(d_gate_attn),
            per_clip(d_scale_ffn),
            per_clip(d_gate_ffn),
            grad_gain0[None],
            grad_gain1[None],
            grad_gain2[None],
            grad_gain3[None],
            placed,
        ]
    )
    small = low(hold(sum_over(small, t_axis, "y", "p"), qkv_summed))
    small_x = pair_stack(small[None], "x", 0)
    small = pair_stack(small_x[None], g_axis, 0)
    rows_low = low(
        jnp.concatenate(
            [outer_reduce(v.reshape(outer, -1, D // 4)) for v in (hold(down_sum, qkv_core), hold(out_sum, qkv_core))]
        )
    )

    rows_done = finish(hold(rows_low, small_x), 1)
    grad_down, grad_out = rows_done[: down_weight.shape[0]], rows_done[down_weight.shape[0] :]
    count = 4 * CLIPS
    d_mod = jnp.concatenate([small[:, :, CLIPS * i : CLIPS * (i + 1)] for i in range(4)], -1).reshape(-1, 4 * D)
    grad_ada = dot(cond_all, d_mod, ((0,), (0,)))
    grad_ada_b = jnp.sum(d_mod.astype(F32), 0)
    sums = jnp.sum(small[:, :, count : count + 8].astype(F32), (0, 1))
    grad_gains = sums[:7]
    grad_head = jnp.sum(sums[7].reshape(HEADS, HEAD), -1) * (1.0 - head_tanh * head_tanh)
    return (
        result,
        input_grad,
        grad_ada,
        grad_ada_b,
        grad_qkv,
        grad_out,
        grad_caption,
        grad_gate_up,
        grad_down,
        grad_null,
        grad_gains,
        grad_head,
    )


def solution(mesh):
    devices = mesh.devices
    outer = devices.shape[1] // 4
    lead = (D // devices.shape[1]) % HEAD != 0
    if lead:
        grid = Mesh(devices.reshape(2, 2, 2, 2, outer), ("x", "core", "p", "y", "o"))
        blk = ("p", "y", "o")
    else:
        grid = Mesh(devices.reshape(2, 2, outer, 2, 2), ("x", "core", "o", "p", "y"))
        blk = ("o", "p", "y")
    dp = ("x", "core")
    every = dp + blk
    in_specs = (
        P(every, None),
        P(every),
        P(None, every),
        P(dp, None),
        P(dp, None, blk),
        P(dp),
        P(None, blk),
        P(blk, None),
        P(),
        P(blk, None),
        P(blk, None),
        P(blk, None),
        P(blk, None),
        P(blk, None),
        P(),
        P(),
        P(every, None),
    )
    out_specs = (
        P(every, None),
        P(every, None),
        P(blk, None),
        P(),
        P(blk, None),
        P(blk, None),
        P(blk, None),
        P(blk, None),
        P(blk, None),
        P(None, blk),
        P(),
        P(),
    )
    return jax.shard_map(
        functools.partial(on_device, outer, lead),
        mesh=grid,
        in_specs=in_specs,
        out_specs=out_specs,
        check_vma=False,
    )
```

```python
import functools

import jax
import jax.numpy as jnp
from jax import lax
from jax.experimental import pallas as pl
from jax.experimental.pallas import tpu as pltpu
from jax.sharding import Mesh, PartitionSpec as P

HEADS = 24
HEAD = 64
D = 1536
FF = 4096
CAP = 128
CLIPS = 2
PAIR = 2 * HEAD

PRECISE = lax.Precision.HIGHEST
EPSILON = 1e-06
NEGATIVE = -1e30
F32 = jnp.float32
LOW = jnp.bfloat16
SWAP = [(0, 1), (1, 0)]


def inv_root(values):
    return lax.rsqrt(jnp.mean(values * values, -1, keepdims=True) + EPSILON)


def unit_rows(values):
    return values * inv_root(values)


def norm_back(grad_in, values, gain):
    root = inv_root(values)
    normed = values * root
    inner = grad_in * gain
    back = root * (inner - normed * jnp.mean(inner * normed, -1, keepdims=True))
    return back, jnp.sum(grad_in * normed, 0)


def rounded(values):
    return lax.reduce_precision(values, 8, 7)


def low(values):
    return rounded(values).astype(LOW)


def dot(a, b, dims=((1,), (0,))):
    return lax.dot_general(a, b, (dims, ((), ())), preferred_element_type=F32)


def nt(a, b):
    return lax.dot_general(a, b, (((1,), (1,)), ((), ())), preferred_element_type=F32)


def tn(a, b):
    return lax.dot_general(a, b, (((0,), (0,)), ((), ())), preferred_element_type=F32)


def nn(a, b):
    return lax.dot_general(a, b, (((1,), (0,)), ((), ())), preferred_element_type=F32)


def cross_bias(seg_col, count):
    clip = lax.broadcasted_iota(jnp.int32, (1, count), 1) // CAP
    return jnp.where(seg_col == clip, 0.0, NEGATIVE)


def forward_near(q_ref, k_ref, v_ref, ck_ref, cv_ref, sq_ref, sk_ref, o_ref, oc_ref, st_ref):
    seg_col = sq_ref[...]
    bias = jnp.where(seg_col == sk_ref[...], 0.0, NEGATIVE)
    bias_cross = cross_bias(seg_col, ck_ref.shape[0])
    for h in range(2):
        at = slice(h * HEAD, (h + 1) * HEAD)
        q = q_ref[:, at]
        s = nt(q, k_ref[:, at]) + bias
        m = jnp.max(s, -1, keepdims=True)
        e = jnp.exp(s - m)
        st_ref[0, :, h : h + 1] = m
        st_ref[0, :, 2 + h : 3 + h] = jnp.sum(e, -1, keepdims=True)
        o_ref[:, at] = nn(e.astype(LOW), v_ref[:, at])
        s = nt(q, ck_ref[:, at]) + bias_cross
        m = jnp.max(s, -1, keepdims=True)
        e = jnp.exp(s - m)
        total = jnp.sum(e, -1, keepdims=True)
        st_ref[0, :, 4 + h : 5 + h] = m + jnp.log(total)
        oc_ref[:, at] = nn(e.astype(LOW), cv_ref[:, at]) / total


def forward_far(
    count, q_ref, k_ref, v_ref, sq_ref, sk_ref, o_ref, oc_ref, st_ref, gate_ref, os_ref, mix_ref, lse_ref, m_ref, l_ref
):
    step = pl.program_id(1)

    @pl.when(step == 0)
    def _():
        os_ref[...] = o_ref[...]
        m_ref[...] = st_ref[0, :, 0:2]
        l_ref[...] = st_ref[0, :, 2:4]

    bias = jnp.where(sq_ref[...] == sk_ref[0], 0.0, NEGATIVE)
    for h in range(2):
        at = slice(h * HEAD, (h + 1) * HEAD)
        s = nt(q_ref[:, at], k_ref[0, :, at]) + bias
        before = m_ref[:, h : h + 1]
        m = jnp.maximum(before, jnp.max(s, -1, keepdims=True))
        e = jnp.exp(s - m)
        factor = jnp.exp(before - m)
        m_ref[:, h : h + 1] = m
        l_ref[:, h : h + 1] = l_ref[:, h : h + 1] * factor + jnp.sum(e, -1, keepdims=True)
        os_ref[:, at] = os_ref[:, at] * factor + nn(e.astype(LOW), v_ref[0, :, at])

    @pl.when(step == count - 1)
    def _():
        for h in range(2):
            at = slice(h * HEAD, (h + 1) * HEAD)
            total = l_ref[:, h : h + 1]
            out = os_ref[:, at] / total
            os_ref[:, at] = out
            mix_ref[:, at] = (out + gate_ref[:, at] * oc_ref[:, at]).astype(LOW)
            lse_ref[0, :, h : h + 1] = m_ref[:, h : h + 1] + jnp.log(total)


def backward_far(
    q_ref, g_ref, os_ref, oc_ref, lse_ref, st_ref, gate_ref, k_ref, v_ref, ck_ref, cv_ref, sq_ref, sk_ref,
    dq_ref, dkv_ref, dck_ref, dcv_ref, dh_ref, delta_ref,
):
    step = pl.program_id(1)
    seg_col = sq_ref[...]
    scaling = HEAD**-0.5

    @pl.when(step == 0)
    def _():
        bias_cross = cross_bias(seg_col, ck_ref.shape[0])
        g = g_ref[...].astype(F32)
        dh_ref[...] = jnp.sum(g * oc_ref[...], 0, keepdims=True)
        for h in range(2):
            at = slice(h * HEAD, (h + 1) * HEAD)
            gh = g[:, at]
            delta_ref[0, :, h : h + 1] = jnp.sum(gh * os_ref[:, at], -1, keepdims=True)
            gc = (gate_ref[:, at] * gh).astype(LOW)
            delta = jnp.sum(gc.astype(F32) * oc_ref[:, at], -1, keepdims=True)
            q = q_ref[:, at]
            p = jnp.exp(nt(q, ck_ref[:, at]) + bias_cross - st_ref[0, :, 4 + h : 5 + h])
            ds = (p * (nt(gc, cv_ref[:, at]) - delta)).astype(LOW)
            dq_ref[:, at] = nn(ds, ck_ref[:, at]) * scaling
            dck_ref[:, at] = tn(ds, q).astype(dck_ref.dtype)
            dcv_ref[:, at] = tn(p.astype(LOW), gc).astype(dcv_ref.dtype)

    bias = jnp.where(seg_col == sk_ref[0], 0.0, NEGATIVE)
    for h in range(2):
        at = slice(h * HEAD, (h + 1) * HEAD)
        q = q_ref[:, at]
        g = g_ref[:, at]
        k = k_ref[0, :, at]
        p = jnp.exp(nt(q, k) + bias - lse_ref[0, :, h : h + 1])
        ds = (p * (nt(g, v_ref[0, :, at]) - delta_ref[0, :, h : h + 1])).astype(LOW)
        dq_ref[:, at] += nn(ds, k) * scaling
        dkv_ref[0, 0, :, at] = tn(ds, q).astype(LOW)
        dkv_ref[0, 1, :, at] = tn(p.astype(LOW), g).astype(LOW)


def backward_near(q_ref, g_ref, lse_ref, delta_ref, k_ref, v_ref, sq_ref, sk_ref, dp_ref, dq_ref, dk_ref, dv_ref):
    bias = jnp.where(sq_ref[...] == sk_ref[...], 0.0, NEGATIVE)
    scaling = HEAD**-0.5
    for h in range(2):
        at = slice(h * HEAD, (h + 1) * HEAD)
        q = q_ref[:, at]
        g = g_ref[:, at]
        k = k_ref[:, at]
        p = jnp.exp(nt(q, k) + bias - lse_ref[0, :, h : h + 1])
        ds = (p * (nt(g, v_ref[:, at]) - delta_ref[0, :, h : h + 1])).astype(LOW)
        dq_ref[:, at] = dp_ref[:, at] + nn(ds, k) * scaling
        dk_ref[:, at] = tn(ds, q)
        dv_ref[:, at] = tn(p.astype(LOW), g)


def swapped(x):
    lane = lax.broadcasted_iota(jnp.int32, x.shape, 1)
    return jnp.where(lane % 2 == 0, pltpu.roll(x, x.shape[1] - 1, 1), pltpu.roll(x, 1, 1))


def heads_in(q_ref, k_ref, v_ref, inv_ref, gq_ref, gk_ref, cos_ref, sin_ref, q_out, kv_out):
    cosine, sine = cos_ref[...], sin_ref[...]
    q = q_ref[...] * inv_ref[:, 0:1] * gq_ref[...]
    k = k_ref[...] * inv_ref[:, 1:2] * gk_ref[...]
    q = (q * cosine + swapped(q) * sine).astype(LOW)
    q_out[...] = (q.astype(F32) * HEAD**-0.5).astype(LOW)
    kv_out[0] = (k * cosine + swapped(k) * sine).astype(LOW)
    kv_out[1] = v_ref[...].astype(LOW)


def heads_back(
    dq_ref, dk_ref, far_ref, q_ref, k_ref, inv_ref, gq_ref, gk_ref, cos_ref, sin_ref, iq_out, ik_out, st_out, gg_out
):
    cosine, sine = cos_ref[...], sin_ref[...]
    dq = dq_ref[...]
    dk = dk_ref[...] + far_ref[0].astype(F32)
    uq = q_ref[...] * inv_ref[:, 0:1]
    uk = k_ref[...] * inv_ref[:, 1:2]
    tq = dq * cosine - swapped(dq) * sine
    tk = dk * cosine - swapped(dk) * sine
    gg_out[0:1] = jnp.sum(tq * uq, 0, keepdims=True)
    gg_out[1:2] = jnp.sum(tk * uk, 0, keepdims=True)
    iq = tq * gq_ref[...]
    ik = tk * gk_ref[...]
    iq_out[...] = iq
    ik_out[...] = ik
    st_out[0, :, 0:1] = jnp.sum(iq * uq, -1, keepdims=True)
    st_out[0, :, 1:2] = jnp.sum(ik * uk, -1, keepdims=True)


def head_calls(tokens, width):
    pairs = width // PAIR
    sds = jax.ShapeDtypeStruct

    def at(first):
        return pl.BlockSpec((tokens, PAIR), lambda i: (0, first + i))

    row = pl.BlockSpec((1, PAIR), lambda i: (0, i))
    fixed = pl.BlockSpec((tokens, PAIR), lambda i: (0, 0))
    inv = pl.BlockSpec((tokens, 2), lambda i: (0, 0))
    both = pl.BlockSpec((2, tokens, PAIR), lambda i: (0, 0, i))
    cost = pl.CostEstimate(flops=20 * tokens * width, bytes_accessed=20 * tokens * width, transcendentals=0)
    into = pl.pallas_call(
        heads_in,
        grid=(pairs,),
        in_specs=[at(0), at(pairs), at(2 * pairs), inv, row, row, fixed, fixed],
        out_specs=[at(0), both],
        out_shape=[sds((tokens, width), LOW), sds((2, tokens, width), LOW)],
        cost_estimate=cost,
        name="heads_in",
    )
    back = pl.pallas_call(
        heads_back,
        grid=(pairs,),
        in_specs=[at(0), at(0), pl.BlockSpec((1, tokens, PAIR), lambda i: (0, 0, i)), at(0), at(pairs), inv, row, row, fixed, fixed],
        out_specs=[at(0), at(0), pl.BlockSpec((1, tokens, 2), lambda i: (i, 0, 0)), pl.BlockSpec((2, PAIR), lambda i: (0, i))],
        out_shape=[sds((tokens, width), F32), sds((tokens, width), F32), sds((pairs, tokens, 2), F32), sds((2, width), F32)],
        cost_estimate=cost,
        name="heads_back",
    )
    return into, back


def place_columns(place, groups, outer, rest, lead):
    whole = 4 * outer * rest
    return [
        g * whole + ((place * outer + o) if lead else (o * 4 + place)) * rest for g in range(groups) for o in range(outer)
    ]


def cut_kernel(columns, rest, me_ref, x_ref, *outs):
    for me in range(4):

        @pl.when(me_ref[0] == me)
        def _():
            for r, out in enumerate(outs):
                for j, start in enumerate(columns[me ^ r]):
                    out[:, j * rest : (j + 1) * rest] = x_ref[:, start : start + rest]


def lay_kernel(columns, rest, blank, me_ref, *refs):
    ins, out = refs[:-1], refs[-1]
    if blank:
        out[...] = jnp.zeros_like(out)
    for me in range(4):

        @pl.when(me_ref[0] == me)
        def _():
            for r, value in enumerate(ins):
                for j, start in enumerate(columns[me ^ r]):
                    out[:, start : start + rest] = value[:, j * rest : (j + 1) * rest]


def caption_kernel(columns, rest, rows_ref, weight_ref, out_ref):
    product = nn(rows_ref[...], weight_ref[...])
    for place in range(4):
        for j, start in enumerate(columns[place]):
            out_ref[place, :, j * rest : (j + 1) * rest] = product[:, start : start + rest].astype(out_ref.dtype)


def assemble_kernel(plan, width, at_ref, *refs):
    ins, out, sems = refs[:-2], refs[-2], refs[-1]
    copies = []
    for i, (source, first, rows) in enumerate(plan):
        row = pl.multiple_of(at_ref[2 * i], 16)
        col = pl.multiple_of(at_ref[2 * i + 1], 128)
        copies.append(
            pltpu.make_async_copy(
                ins[source].at[pl.ds(first, rows)], out.at[pl.ds(row, rows), pl.ds(col, width)], sems.at[i]
            )
        )
    for copy in copies:
        copy.start()
    for copy in copies:
        copy.wait()


def product_kernel(left_ref, right_ref, out_ref):
    out_ref[0] = tn(left_ref[...], right_ref[...]).astype(out_ref.dtype)


def grad_product(left, right, parts):
    rows, cols = left.shape[1], right.shape[1] // parts
    tile = 512 if rows % 512 == 0 else rows
    return pl.pallas_call(
        product_kernel,
        grid=(parts, rows // tile),
        in_specs=[
            pl.BlockSpec((left.shape[0], tile), lambda q, i: (0, i)),
            pl.BlockSpec((left.shape[0], cols), lambda q, i: (0, q)),
        ],
        out_specs=pl.BlockSpec((1, tile, cols), lambda q, i: (q, i, 0)),
        out_shape=jax.ShapeDtypeStruct((parts, rows, cols), LOW),
        cost_estimate=pl.CostEstimate(
            flops=2 * left.shape[0] * rows * right.shape[1],
            bytes_accessed=2 * (rows * right.shape[1] + left.size + right.size),
            transcendentals=0,
        ),
        compiler_params=pltpu.CompilerParams(fuse_transposed_lhs_in_matmul=True),
        name="grad_product",
    )(left, right)


def assemble(inputs, plan, places, shape):
    width = inputs[0].shape[1]
    at = jnp.stack([jnp.asarray(v, jnp.int32) for pair in places for v in pair])
    size = 2 * shape[0] * shape[1] * 2
    return pl.pallas_call(
        functools.partial(assemble_kernel, plan, width),
        grid_spec=pltpu.PrefetchScalarGridSpec(
            num_scalar_prefetch=1,
            grid=(1,),
            in_specs=[pl.BlockSpec(memory_space=pl.ANY)] * len(inputs),
            out_specs=pl.BlockSpec(memory_space=pltpu.VMEM),
            scratch_shapes=[pltpu.SemaphoreType.DMA((len(plan),))],
        ),
        out_shape=jax.ShapeDtypeStruct(shape, inputs[0].dtype),
        compiler_params=pltpu.CompilerParams(vmem_limit_bytes=32 * 1024 * 1024),
        cost_estimate=pl.CostEstimate(flops=0, bytes_accessed=size, transcendentals=0),
        name="assemble",
    )(at, *inputs)


def attention_calls(tokens, width, capt, far):
    pairs = width // PAIR
    sds = jax.ShapeDtypeStruct

    def cols(rows):
        return pl.BlockSpec((rows, PAIR), lambda i, *r: (0, i))

    def stat(n):
        return pl.BlockSpec((1, tokens, n), lambda i, *r: (i, 0, 0))

    seg_col = pl.BlockSpec((tokens, 1), lambda i, *r: (0, 0))
    seg_row = pl.BlockSpec((1, tokens), lambda i, *r: (0, 0))
    far_k = pl.BlockSpec((1, None, tokens, PAIR), lambda i, r: (r, 0, 0, i))
    far_v = pl.BlockSpec((1, None, tokens, PAIR), lambda i, r: (r, 1, 0, i))
    far_both = pl.BlockSpec((1, 2, tokens, PAIR), lambda i, r: (r, 0, 0, i))
    near_k = pl.BlockSpec((None, tokens, PAIR), lambda i, *r: (0, 0, i))
    near_v = pl.BlockSpec((None, tokens, PAIR), lambda i, *r: (1, 0, i))
    far_row = pl.BlockSpec((1, 1, tokens), lambda i, r: (r, 0, 0))
    gate = cols(1)
    tok, cap = cols(tokens), cols(capt)

    def cost(keys, products):
        return pl.CostEstimate(
            flops=2 * tokens * keys * width * products,
            bytes_accessed=8 * tokens * width * 4,
            transcendentals=tokens * keys * (width // HEAD),
        )

    params = pltpu.CompilerParams(vmem_limit_bytes=48 * 1024 * 1024)
    near = pl.pallas_call(
        forward_near,
        grid=(pairs,),
        in_specs=[tok, near_k, near_v, cap, cap, seg_col, seg_row],
        out_specs=[tok, tok, stat(8)],
        out_shape=[sds((tokens, width), F32), sds((tokens, width), F32), sds((pairs, tokens, 8), F32)],
        compiler_params=params,
        cost_estimate=cost(tokens + capt, 2),
        name="attn_near",
    )
    away = pl.pallas_call(
        functools.partial(forward_far, far),
        grid=(pairs, far),
        in_specs=[tok, far_k, far_v, seg_col, far_row, tok, tok, stat(8), gate],
        out_specs=[tok, tok, stat(2)],
        out_shape=[sds((tokens, width), F32), sds((tokens, width), LOW), sds((pairs, tokens, 2), F32)],
        scratch_shapes=[pltpu.VMEM((tokens, 2), F32), pltpu.VMEM((tokens, 2), F32)],
        compiler_params=params,
        cost_estimate=cost(tokens * far, 2),
        name="attn_far",
    )
    back_away = pl.pallas_call(
        backward_far,
        grid=(pairs, far),
        in_specs=[tok, tok, tok, tok, stat(2), stat(8), gate, far_k, far_v, cap, cap, seg_col, far_row],
        out_specs=[tok, far_both, cap, cap, gate, stat(2)],
        out_shape=[
            sds((tokens, width), F32),
            sds((far, 2, tokens, width), LOW),
            sds((capt, width), F32),
            sds((capt, width), F32),
            sds((1, width), F32),
            sds((pairs, tokens, 2), F32),
        ],
        compiler_params=params,
        cost_estimate=cost(tokens * far + capt, 5),
        name="attn_back_far",
    )
    back_near = pl.pallas_call(
        backward_near,
        grid=(pairs,),
        in_specs=[tok, tok, stat(2), stat(2), near_k, near_v, seg_col, seg_row, tok],
        out_specs=[tok, tok, tok],
        out_shape=[sds((tokens, width), F32)] * 3,
        compiler_params=params,
        cost_estimate=cost(tokens, 5),
        name="attn_back_near",
    )
    return near, away, back_away, back_near


def swap(value, axis):
    return lax.ppermute(value, axis, SWAP)


def pair_stack(value, axis, dim):
    other = swap(value, axis)
    first = lax.axis_index(axis) == 0
    return jnp.concatenate([jnp.where(first, value, other), jnp.where(first, other, value)], dim)


def hold(value, *after):
    return lax.optimization_barrier((value, after))[0]


def on_device(
    outer,
    lead,
    hidden,
    segments,
    positions,
    condition,
    captions,
    dropped,
    null_caption,
    ada_weight,
    ada_bias,
    qkv_weight,
    out_weight,
    caption_weight,
    gate_up,
    down_weight,
    gains,
    head_gate,
    cotangent,
):
    me_c = lax.axis_index("p") * 2 + lax.axis_index("y")
    me_o = lax.axis_index("o")
    core = lax.axis_index("core")
    me_x = lax.axis_index("x")
    me_b = lax.axis_index(("p", "y", "o") if lead else ("o", "p", "y"))
    me_arg = me_c.reshape(1).astype(jnp.int32)
    tokens = hidden.shape[0]
    square = 4 * tokens
    width = D // 4
    capt = CLIPS * CAP
    blk = 4 * outer
    rest = D // blk
    mirrored = outer == 2
    t_axis, g_axis = ("core", "o") if mirrored else ("o", "core")
    t_size = 2 if mirrored else outer
    me_t, me_g = lax.axis_index(t_axis), lax.axis_index(g_axis)
    across = [[(i, i ^ r) for i in range(4)] for r in range(4)]
    beyond = [[(i, i ^ r) for i in range(outer)] for r in range(outer)]

    def unblocks(value):
        if lead:
            value = value.swapaxes(-3, -2)
        return value.reshape(value.shape[:-3] + (-1,))

    def row_blocks(value):
        size = value.shape[0] // blk
        if lead:
            return value.reshape((4, outer, size) + value.shape[1:]).swapaxes(0, 1)
        return value.reshape((outer, 4, size) + value.shape[1:])

    def block_index(o, c):
        return c * outer + o if lead else o * 4 + c

    def cut(value, groups, count):
        size = value.shape[1] // (groups * blk)
        columns = [place_columns(c, groups, outer, size, lead) for c in range(4)]
        out = jax.ShapeDtypeStruct((value.shape[0], groups * outer * size), value.dtype)
        return pl.pallas_call(
            functools.partial(cut_kernel, columns, size),
            in_specs=[pl.BlockSpec(memory_space=pltpu.SMEM), pl.BlockSpec(memory_space=pltpu.VMEM)],
            out_specs=[pl.BlockSpec(memory_space=pltpu.VMEM)] * count,
            out_shape=[out] * count,
            name="cut",
        )(me_arg, value)

    def lay(pieces, groups):
        size = pieces[0].shape[1] // (groups * outer)
        columns = [place_columns(c, groups, outer, size, lead) for c in range(4)]
        shape = (pieces[0].shape[0], 4 * pieces[0].shape[1])
        return pl.pallas_call(
            functools.partial(lay_kernel, columns, size, len(pieces) < 4),
            in_specs=[pl.BlockSpec(memory_space=pltpu.SMEM)] + [pl.BlockSpec(memory_space=pltpu.VMEM)] * len(pieces),
            out_specs=pl.BlockSpec(memory_space=pltpu.VMEM),
            out_shape=jax.ShapeDtypeStruct(shape, pieces[0].dtype),
            name="lay",
        )(me_arg, *pieces)

    def outer_reduce(value):
        if outer == 2:
            sent = lax.dynamic_index_in_dim(value, 1 - me_o, 0, keepdims=False).astype(LOW)
            kept = lax.dynamic_index_in_dim(value, me_o, 0, keepdims=False)
            return kept.astype(F32) + swap(sent, "o").astype(F32)
        return lax.psum_scatter(value.astype(LOW), "o", scatter_dimension=0).astype(F32)

    def axis_sum(value, axis):
        if axis != "o" or outer == 2:
            return rounded(value) + swap(low(value), axis).astype(F32)
        return lax.psum(low(value), axis).astype(F32)

    def mirror(value):
        if not mirrored:
            return value
        other = lax.ppermute(value, ("core", "o"), [(1, 2), (2, 1)])
        return jnp.where(core == me_o, value, other)

    def far(value):
        return jnp.stack([lax.ppermute(value, t_axis, [(i, i ^ r) for i in range(t_size)]) for r in range(1, t_size)])

    def to_place(value, r):
        return lax.ppermute(value, ("p", "y"), across[r])

    def gather_places(rows):
        return [rows] + [to_place(rows, r) for r in (1, 2, 3)]

    def gather_square(rows):
        return jnp.concatenate(gather_places(rows))

    def scatter_places(parts):
        total = parts[0]
        for r in (1, 2, 3):
            total = total + to_place(parts[r].astype(LOW), r).astype(F32)
        return total

    def scatter_square(full):
        return scatter_places([full[r * tokens : (r + 1) * tokens] for r in range(4)])

    def square_sum(value, shared=None):
        count = 4 * value.shape[0]
        whole = value.reshape(count, tokens)
        if shared is not None:
            whole = jnp.concatenate([whole, shared.reshape(-1, tokens)])
        for axis, order in (("y", (1, 0, 3, 2)), ("p", (2, 3, 0, 1))):
            other = swap(whole, axis)
            order = [4 * i + j for i in range(value.shape[0]) for j in order]
            whole = whole + jnp.concatenate([other[i : i + 1] for i in order] + [other[count:]])
        sums = whole[:count].reshape(value.shape)
        return sums if shared is None else (sums, whole[count:].reshape(-1))

    def sum_over(value, *axes):
        for axis in axes:
            value = axis_sum(value, axis)
        return value

    def hand_on(own, split):
        pieces = [(own, 0, 0, 0)]
        if split:
            pieces += [(swap(own, "x"), 0, 1, 0)]
        for r in range(1, outer):
            far_piece = lax.ppermute(own, "o", beyond[r])
            pieces += [(far_piece, 0, 0, r)]
            if split:
                pieces += [(swap(far_piece, "x"), 0, 1, r)]
        if split:
            other = swap(jnp.concatenate([piece[0] for piece in pieces]), "core")
            size = own.shape[0]
            pieces += [(other[i * size : (i + 1) * size], 1, x, o) for i, (_, _, x, o) in enumerate(pieces)]
        return pieces

    def fetch_qkv(weight, after):
        rows = weight.shape[0]
        split = (rows // 4) % 16 == 0
        quarter = rows // 4 if split else rows
        if split:
            weight = lax.dynamic_slice_in_dim(weight, (me_x * 2 + core) * quarter, quarter, 0)
        cuts = cut(weight, 3, 4)
        arrived = [to_place(cuts[r], r) for r in (1, 2, 3)]
        pieces = hand_on(hold(jnp.concatenate([cuts[0]] + arrived), after), split)
        plan, places = [], []
        for i, (_, k, x, o) in enumerate(pieces):
            for r in range(4):
                plan.append((i, r * quarter, quarter))
                at = block_index(me_o ^ o, me_c ^ r) * rows
                places.append((at + ((me_x ^ x) * 2 + (core ^ k)) * quarter if split else at, 0))
        whole = assemble([piece[0] for piece in pieces], plan, places, (D, 3 * D // 4))
        return whole, pieces, arrived

    def start_gate_up(weight):
        rows = weight.shape[0]
        f = FF // blk

        def piece_of(r):
            cols = []
            for j in range(outer // 2):
                o = me_x * (outer // 2) + j
                at = core * FF + block_index(o, me_c ^ r) * f
                cols.append(lax.dynamic_slice(weight, (0, at), (rows, f)))
            return jnp.concatenate(cols, 1) if len(cols) > 1 else cols[0]

        arrived = [to_place(piece_of(r), r) for r in (1, 2, 3)]
        own = jnp.concatenate([piece_of(0)] + arrived)
        return own, arrived

    def fetch_gate_up(own):
        rows, n = own.shape[0] // 4, own.shape[1]
        whole = lax.all_gather(own, ("core", "x", "o"), axis=0, tiled=True)
        plan, places = [], []
        for q in range(4):
            for o in range(outer):
                for r in range(4):
                    plan.append((0, ((q * outer + o) * 4 + r) * rows, rows))
                    places.append((block_index(o, me_c ^ r) * rows, q * n))
        return assemble([whole], plan, places, (D, 2 * FF // 4))

    def fetch_down(weight, after):
        rows, quarter = weight.shape[0], D // 4
        mine = lax.dynamic_slice(weight, (0, (core * 2 + me_x) * quarter), (rows, quarter))
        whole = lax.all_gather(hold(mine, after), ("core", "x", "o"), axis=0, tiled=True)
        plan = [(0, i * rows, rows) for i in range(4 * outer)]
        places = [(o * rows, q * quarter) for q in range(4) for o in range(outer)]
        return assemble([whole], plan, places, (outer * rows, D))

    def fetch_rows(weight):
        rows, quarter = weight.shape[0], D // 4
        mine = lax.dynamic_slice(weight, (0, (core * 2 + me_x) * quarter), (rows, quarter))
        pieces = hand_on(mine, True)
        plan = [(i, 0, rows) for i in range(len(pieces))]
        places = [((me_o ^ o) * rows, ((core ^ k) * 2 + (me_x ^ x)) * quarter) for _, k, x, o in pieces]
        return assemble([piece[0] for piece in pieces], plan, places, (outer * rows, D)), pieces

    def finish(part, dim):
        return pair_stack(pair_stack(part, "x", dim), "core", dim).astype(F32)

    def two_cores(value):
        return jnp.concatenate([value, swap(value, "core")])

    def two_cores_half(value):
        half = value.shape[1] // 2
        first = core == 0
        a, b = value[:, :half], value[:, half:]
        return jnp.concatenate([jnp.where(first, a, b), swap(jnp.where(first, b, a), "core")])

    def grad_columns(left_both, grad_both):
        half = grad_both.shape[1] // 2
        theirs = lax.dynamic_slice_in_dim(grad_both, (1 - me_x) * half, half, 1)
        mine = lax.dynamic_slice_in_dim(grad_both, me_x * half, half, 1)
        sent = swap(dot(left_both, theirs, ((0,), (0,))).astype(LOW), "x")
        return dot(left_both, mine, ((0,), (0,))) + sent.astype(F32)

    numbers = jnp.concatenate([segments[None], positions]).T.astype(LOW)
    numbers = jnp.pad(numbers, ((0, 0), (0, 128 - numbers.shape[1])))
    mine = mirror(jnp.concatenate([hidden, numbers], 1))
    source = mine[:, :D].astype(F32)
    segment_here = mine[:, D].astype(jnp.int32)
    chosen = jnp.where(dropped[:, None, None] == 1, null_caption[None], captions)
    chosen_rows = chosen.reshape(capt, chosen.shape[2])
    caption_parts = pl.pallas_call(
        functools.partial(caption_kernel, [place_columns(c, 2, outer, rest, lead) for c in range(4)], rest),
        out_shape=jax.ShapeDtypeStruct((4, capt, 2 * width), LOW),
        in_specs=[pl.BlockSpec(memory_space=pltpu.VMEM)] * 2,
        out_specs=pl.BlockSpec(memory_space=pltpu.VMEM),
        compiler_params=pltpu.CompilerParams(vmem_limit_bytes=40 * 1024 * 1024),
        cost_estimate=pl.CostEstimate(
            flops=2 * capt * chosen_rows.shape[1] * 2 * D, bytes_accessed=8 * 1024 * 1024, transcendentals=0
        ),
        name="caption_product",
    )(chosen_rows, caption_weight)
    caption_parts = [lax.dynamic_index_in_dim(caption_parts, me_c ^ r, 0, keepdims=False) for r in range(4)]
    caption_half = scatter_places([caption_parts[0].astype(F32)] + caption_parts[1:])

    cond_rows = ada_weight.shape[0]
    cond_low = lax.dynamic_slice_in_dim(jax.nn.silu(condition), me_b * cond_rows, cond_rows, 1).astype(LOW)
    cond_both = pair_stack(cond_low, "core", 0)
    cond_all = pair_stack(cond_both.reshape(2, 1, CLIPS, cond_rows), "x", 1).reshape(-1, cond_rows)
    modulation = sum_over(dot(cond_both, ada_weight), "o", "y", "p")
    modulation = lax.dynamic_slice_in_dim(modulation, me_g * CLIPS, CLIPS, 0) + ada_bias
    qkv_mine, qkv_pieces, qkv_arrived = fetch_qkv(qkv_weight, caption_half)
    tokens_blocks = gather_places(hold(mine, qkv_arrived, modulation))
    tokens_square = jnp.concatenate(tokens_blocks)
    hidden_square = tokens_square[:, :D].astype(F32)
    seg_square = tokens_square[:, D].astype(jnp.int32)
    pos_square = tokens_square[:, D + 1 : D + 4].astype(F32)
    seg_col, seg_row = seg_square[:, None], seg_square[None]
    seg_far = far(seg_row)

    qkv_here = qkv_pieces[2][0] if outer == 2 else qkv_pieces[-1][0]


    up_own, up_arrived = start_gate_up(hold(gate_up, tokens_blocks[3]))
    up_own = hold(up_own, qkv_here)


    head_tanh = jnp.tanh(head_gate)
    (place_gains,) = cut(jnp.concatenate([gains[4:7], jnp.repeat(head_tanh, HEAD)[None]]), 1, 1)
    gain_q, gain_k, gain_c, gate_row = (place_gains[i : i + 1] for i in range(4))

    pair_index = jnp.arange(PAIR) % HEAD // 2
    frequency = 10000.0 ** (-3.0 * (pair_index // 3).astype(F32) / (HEAD // 2))
    select = ((pair_index % 3)[None, :] == jnp.arange(3)[:, None]).astype(F32)
    angles = jnp.dot(pos_square, select, precision=PRECISE) * frequency[None, :]
    cosine = jnp.cos(angles)
    sine = jnp.sin(angles) * jnp.where(jnp.arange(PAIR) % 2 == 0, -1.0, 1.0)[None]

    def per_token(rows, sel):
        return jnp.where(sel, rows[0:1], rows[1:2])

    caption_mine = axis_sum(mirror(hold(caption_half, qkv_here).astype(LOW)).astype(F32), t_axis)
    scale_square = per_token(hold(modulation[:, :D], up_arrived, caption_mine, cosine), seg_col == 0)
    first_in = (unit_rows(hidden_square) * gains[0] * (1.0 + scale_square)).astype(LOW)
    projected = dot(first_in, qkv_mine)
    q_raw, k_raw = projected[:, :width], projected[:, width : 2 * width]
    ck_raw = caption_mine[:, :width]
    sums, sums_c = square_sum(
        jnp.stack([jnp.sum(q_raw * q_raw, -1), jnp.sum(k_raw * k_raw, -1)]), jnp.sum(ck_raw * ck_raw, -1)
    )
    outw, out_pieces = fetch_rows(hold(out_weight, qkv_here))
    gate_up_mine = fetch_gate_up(up_own)
    down_mine = fetch_down(down_weight, projected)
    inv = hold(lax.rsqrt(sums / D + EPSILON).T, seg_far, out_pieces[2][0])
    heads_into, heads_out = head_calls(square, width)
    queries, kv = heads_into(projected, projected, projected, inv, gain_q, gain_k, cosine, sine)
    inv_c = lax.rsqrt(sums_c / D + EPSILON)[:, None]
    unit_c = ck_raw * inv_c
    cap_keys = (unit_c * gain_c).astype(LOW)
    cap_values = caption_mine[:, width:].astype(LOW)
    kv_far = far(kv)

    near, away, back_away, back_near = attention_calls(square, width, capt, t_size - 1)
    out_near, out_cross, stats = near(queries, kv, kv, cap_keys, cap_values, seg_col, seg_row)
    out_self, mixed, lse = away(queries, kv_far, kv_far, seg_col, seg_far, out_near, out_cross, stats, gate_row)
    mixed_both = two_cores(mixed)
    attended = scatter_square(dot(mixed, outw))

    clip_here = segment_here[:, None] == 0
    scale_attn = per_token(modulation[:, :D], clip_here)
    gate_attn = jnp.tanh(per_token(modulation[:, D : 2 * D], clip_here))
    scale_ffn = per_token(modulation[:, 2 * D : 3 * D], clip_here)
    gate_ffn = jnp.tanh(per_token(modulation[:, 3 * D :], clip_here))
    attn_unit = unit_rows(attended)
    middle = source + gate_attn * attn_unit * gains[1]
    unit_mid = unit_rows(middle)
    second_low = (unit_mid * gains[2] * (1.0 + scale_ffn)).astype(LOW)
    second_in = gather_square(second_low)
    hidden_units = FF // 4
    gate_values = dot(second_in, gate_up_mine)
    gate_part, up_part = gate_values[:, :hidden_units], gate_values[:, hidden_units:]
    activated = (jax.nn.silu(gate_part) * up_part).astype(LOW)
    activated_both = two_cores(activated)
    lowered = scatter_square(dot(activated, down_mine))
    low_unit = unit_rows(lowered)
    result = middle + gate_ffn * low_unit * gains[3]

    upstream = mirror(cotangent).astype(F32)
    d_gate_ffn = upstream * low_unit * gains[3] * (1.0 - gate_ffn * gate_ffn)
    d_lowered, grad_gain3 = norm_back(upstream * gate_ffn, lowered, gains[3])
    d_lowered_sq = gather_square(d_lowered.astype(LOW))
    d_activated = dot(d_lowered_sq, down_mine, ((1,), (1,)))
    sigmoid = jax.nn.sigmoid(gate_part)
    d_gate_part = d_activated * up_part * sigmoid * (1.0 + gate_part * (1.0 - sigmoid))
    d_up_part = d_activated * gate_part * sigmoid
    d_gate_values = jnp.concatenate([d_gate_part, d_up_part], 1).astype(LOW)
    d_second = scatter_square(dot(d_gate_values, gate_up_mine, ((1,), (1,))))

    down_sum = grad_columns(activated_both, two_cores_half(d_lowered_sq))
    up_terms = grad_product(second_in, d_gate_values, 4)
    up_terms = jnp.stack([row_blocks(up_terms[q]) for q in range(4)]) if lead else up_terms
    up_terms = up_terms.reshape((4 * outer, D // outer) + up_terms.shape[-1:])
    up_rows = lax.psum_scatter(up_terms, ("core", "x", "o"), scatter_dimension=0)
    up_rows = up_rows.reshape(4, gate_up.shape[0], -1)

    d_scale_ffn = d_second * unit_mid * gains[2]
    d_middle_norm, grad_gain2 = norm_back(d_second * (1.0 + scale_ffn), middle, gains[2])
    d_middle = upstream + d_middle_norm
    d_gate_attn = d_middle * attn_unit * gains[1] * (1.0 - gate_attn * gate_attn)
    d_attended, grad_gain1 = norm_back(d_middle * gate_attn, attended, gains[1])

    d_attended_sq = gather_square(d_attended.astype(LOW))
    d_mixed = dot(d_attended_sq, outw, ((1,), (1,))).astype(LOW)
    dq_part, dkv_far, dck, dcv, d_head, delta = back_away(
        queries, d_mixed, out_self, out_cross, lse, stats, gate_row, kv_far, kv_far, cap_keys,
        cap_values, seg_col, seg_far,
    )
    far_terms = [lax.ppermute(dkv_far[r - 1], t_axis, [(i, i ^ r) for i in range(t_size)]) for r in range(1, t_size)]
    d_query, dk_near, dv_near = back_near(queries, d_mixed, lse, delta, kv, kv, seg_col, seg_row, dq_part)
    dkv_other = far_terms[0] if t_size == 2 else sum(term.astype(F32) for term in far_terms)
    d_cap = axis_sum(jnp.concatenate([dck, dcv], 1), t_axis)
    out_sum = grad_columns(mixed_both, two_cores_half(d_attended_sq))
    inner_q, inner_k, head_sums, gain_qk = heads_out(
        d_query, dk_near, dkv_other, projected, projected, inv, gain_q, gain_k, cosine, sine
    )
    inner_c = d_cap[:, :width] * gain_c
    sums, sums_c = square_sum(jnp.sum(head_sums, 0).T, jnp.sum(inner_c * unit_c, -1))
    mean = (sums / D).T
    d_q_raw = inv[:, 0:1] * (inner_q - q_raw * inv[:, 0:1] * mean[:, 0:1])
    d_k_raw = inv[:, 1:2] * (inner_k - k_raw * inv[:, 1:2] * mean[:, 1:2])
    d_value = dv_near + dkv_other[1].astype(F32)
    d_projected = jnp.concatenate([d_q_raw, d_k_raw, d_value], 1).astype(LOW)
    rows_qkv = qkv_weight.shape[0]
    quarter = rows_qkv // 4
    qkv_part = dot(first_in, d_projected, ((0,), (0,))).astype(LOW)
    qkv_part = row_blocks(qkv_part).reshape(outer, 4, 2, 2, quarter, -1)
    qkv_core = swap(lax.dynamic_index_in_dim(qkv_part, 1 - core, 3, keepdims=False), "core")
    qkv_own = lax.dynamic_index_in_dim(qkv_part, core, 3, keepdims=False)
    qkv_part = (qkv_own.astype(F32) + qkv_core.astype(F32)).astype(LOW)
    qkv_x = swap(lax.dynamic_index_in_dim(qkv_part, 1 - me_x, 2, keepdims=False), "x")
    qkv_own = lax.dynamic_index_in_dim(qkv_part, me_x, 2, keepdims=False)
    qkv_part = (qkv_own.astype(F32) + qkv_x.astype(F32)).astype(LOW)
    d_first = scatter_square(dot(hold(d_projected, qkv_core), qkv_mine, ((1,), (1,))))
    up_rows = hold(up_rows, d_projected)
    half_outer = outer // 2
    f = FF // blk
    up_low = jnp.zeros((gate_up.shape[0], 4 * up_rows.shape[2]), LOW)
    for r in range(4):
        piece = lax.dynamic_index_in_dim(up_rows, me_c ^ r, 0, keepdims=False)
        piece = to_place(piece, r) if r else piece
        for j in range(half_outer):
            up_low = lax.dynamic_update_slice(up_low, piece[:, j * f : (j + 1) * f], (0, (j * 4 + (me_c ^ r)) * f))
    up_half = pair_stack(hold(up_low, qkv_x), "x", 1)
    grad_gate_up = pair_stack(up_half, "core", 1).astype(F32)
    if lead:
        grad_gate_up = unblocks(grad_gate_up.reshape(-1, 2, outer, 4, f)).reshape(gate_up.shape)


    qkv_part = low(outer_reduce(qkv_part))
    qkv_summed = qkv_part
    qkv_part = [lax.dynamic_index_in_dim(qkv_part, me_c ^ r, 0, keepdims=False) for r in range(4)]
    qkv_part = qkv_part[:1] + [to_place(qkv_part[r], r) for r in (1, 2, 3)]
    qkv_part = lay(qkv_part, 3)
    qkv_part = pair_stack(qkv_part[None], "x", 0)
    qkv_other = swap(qkv_part, "core")
    grad_qkv = jnp.stack([jnp.where(core == i, qkv_part, qkv_other) for i in range(2)], 1)
    grad_qkv = grad_qkv.reshape(rows_qkv, -1).astype(F32)


    d_c_raw = inv_c * (inner_c - unit_c * (sums_c / D)[:, None])
    d_cap_mine = jnp.concatenate([d_c_raw, d_cap[:, width:]], 1).astype(LOW)
    cap_blocks = gather_places(hold(mirror(d_cap_mine), qkv_x))
    d_cap_low = lay(cap_blocks, 2)
    grad_caption = finish(low(grad_columns(two_cores(chosen_rows), two_cores_half(d_cap_low))), 1)
    d_chosen = dot(d_cap_low, caption_weight, ((1,), (1,))).reshape(CLIPS, CAP, -1)
    grad_null = jnp.sum(jnp.where(dropped[:, None, None] == 1, d_chosen, 0.0), 0)
    grad_null = rounded(grad_null) + swap(low(grad_null), "core").astype(F32)
    grad_null = rounded(grad_null) + swap(low(grad_null), "x").astype(F32)

    unit_in = unit_rows(source)
    d_scale_attn = d_first * unit_in * gains[0]
    d_source_norm, grad_gain0 = norm_back(d_first * (1.0 + scale_attn), source, gains[0])
    input_grad = d_middle + d_source_norm
    if mirrored:
        input_grad = jnp.where(core == me_o, input_grad, mirror(input_grad.astype(LOW)).astype(F32))
        result = jnp.where(core == me_o, result, mirror(result.astype(LOW)).astype(F32))

    onehot = (segment_here[:, None] == jnp.arange(CLIPS)[None, :]).astype(F32)

    def per_clip(grad):
        return lax.dot_general(onehot, grad, (((0,), (0,)), ((), ())), precision=PRECISE)

    grad_gain6 = jnp.where(me_t == 0, jnp.sum(d_cap[:, :width] * unit_c, 0), 0.0)
    placed = lay([jnp.concatenate([gain_qk, grad_gain6[None], d_head])], 1)
    small = jnp.concatenate(
        [
            per_clip(d_scale_attn),
            per_clip(d_gate_attn),
            per_clip(d_scale_ffn),
            per_clip(d_gate_ffn),
            grad_gain0[None],
            grad_gain1[None],
            grad_gain2[None],
            grad_gain3[None],
            placed,
        ]
    )
    small = low(hold(sum_over(small, t_axis, "y", "p"), qkv_summed))
    small_x = pair_stack(small[None], "x", 0)
    small = pair_stack(small_x[None], g_axis, 0)
    rows_low = low(
        jnp.concatenate(
            [outer_reduce(v.reshape(outer, -1, D // 4)) for v in (hold(down_sum, qkv_core), hold(out_sum, qkv_core))]
        )
    )

    rows_done = finish(hold(rows_low, small_x), 1)
    grad_down, grad_out = rows_done[: down_weight.shape[0]], rows_done[down_weight.shape[0] :]
    count = 4 * CLIPS
    d_mod = jnp.concatenate([small[:, :, CLIPS * i : CLIPS * (i + 1)] for i in range(4)], -1).reshape(-1, 4 * D)
    grad_ada = dot(cond_all, d_mod, ((0,), (0,)))
    grad_ada_b = jnp.sum(d_mod.astype(F32), 0)
    sums = jnp.sum(small[:, :, count : count + 8].astype(F32), (0, 1))
    grad_gains = sums[:7]
    grad_head = jnp.sum(sums[7].reshape(HEADS, HEAD), -1) * (1.0 - head_tanh * head_tanh)
    return (
        result,
        input_grad,
        grad_ada,
        grad_ada_b,
        grad_qkv,
        grad_out,
        grad_caption,
        grad_gate_up,
        grad_down,
        grad_null,
        grad_gains,
        grad_head,
    )


def solution(mesh):
    devices = mesh.devices
    outer = devices.shape[1] // 4
    lead = (D // devices.shape[1]) % HEAD != 0
    if lead:
        grid = Mesh(devices.reshape(2, 2, 2, 2, outer), ("x", "core", "p", "y", "o"))
        blk = ("p", "y", "o")
    else:
        grid = Mesh(devices.reshape(2, 2, outer, 2, 2), ("x", "core", "o", "p", "y"))
        blk = ("o", "p", "y")
    dp = ("x", "core")
    every = dp + blk
    in_specs = (
        P(every, None),
        P(every),
        P(None, every),
        P(dp, None),
        P(dp, None, blk),
        P(dp),
        P(None, blk),
        P(blk, None),
        P(),
        P(blk, None),
        P(blk, None),
        P(blk, None),
        P(blk, None),
        P(blk, None),
        P(),
        P(),
        P(every, None),
    )
    out_specs = (
        P(every, None),
        P(every, None),
        P(blk, None),
        P(),
        P(blk, None),
        P(blk, None),
        P(blk, None),
        P(blk, None),
        P(blk, None),
        P(None, blk),
        P(),
        P(),
    )
    return jax.shard_map(
        functools.partial(on_device, outer, lead),
        mesh=grid,
        in_specs=in_specs,
        out_specs=out_specs,
        check_vma=False,
    )
```
